32 devices in a mesh: node: 4 (over z), space: 8 (over y, x, core).
Axes of the slice: x: 2, y: 2, z: 4, core: 2. Of those that a mesh axis runs over, the one named last changes fastest.
Arguments:
- start_state: float32 [5, 4, 4, 4, 8, 1280], P(None, None, None, None, 'space'), may hold values from -1.5 to 14, as said below
- node_offset: float32 [4, 5, 4, 4, 4, 8, 1280], P('node', None, None, None, None, 'space'), may hold values from -0.6 to 0.6
Outputs:
- increments: float32 [4, 5, 4, 4, 4, 8, 1280], P('node', None, None, None, None, 'space')
The draws below stay inside these ranges and needn't reach their ends.
Inputs may be any that keep to these rules, and one draw needn't show every extreme that they name: `start_state`: conserved variables of a gas with gamma 1.4, density and pressure between 2 and 5 and every velocity component within 0.3 in magnitude, drawn independently at each node.
All inputs are finite; a program needn't handle non-finite values.
Results may differ from the reference program's by a relative error of at most 0.0001.
Values sent between devices are 32-bit elements; how exact they have to be, the bound alone decides.
No kernel may reach another device: no remote copies, remote signals or barrier semaphores. Data moves between devices by JAX's collectives and lax.ppermute only.
A program may use at most 64 MiB of HBM per device.

```python
import math
import jax
import jax.numpy as jnp
import numpy as np
from jax import lax

EY = 16
EZ = 80
BASIS = 4
VARIABLES = 5
TIME_NODES = 4
ITERS = 2
NXE = 8
PLANE = 1280


def draw_start_state(key, part):
    subkeys = jax.random.split(key, 3)
    grid_shape = (4, 4, 4, NXE, PLANE)
    density = jax.random.uniform(subkeys[0], grid_shape, jnp.float32, 2.0, 4.0)
    pressure = jax.random.uniform(subkeys[2], grid_shape, jnp.float32, 2.0, 4.0)
    velocity = jax.random.uniform(subkeys[1], (3,) + grid_shape, jnp.float32, -0.3, 0.3)
    momenta = density * velocity
    energy = pressure / 0.4 + 0.5 * density * jnp.sum(velocity * velocity, axis=0)
    return jnp.concatenate([density[None], momenta, energy[None]], axis=0)


def shard_levels(rng, extent, cuts, smallest, top_value):
    gain = 1.0
    for axis_at, shards_of in cuts:
        steps = jax.random.uniform(jax.random.fold_in(jax.random.fold_in(rng, 6), axis_at), (shards_of,), jnp.float32, smallest / len(cuts), top_value / len(cuts))
        gain = gain * jnp.repeat(jnp.exp(steps), extent[axis_at] // shards_of).reshape((-1,) + (1,) * (len(extent) - 1 - axis_at))
    return gain


def gaussian(key, extent, spread, most, cuts=(), kind=jnp.bfloat16):
    gain = shard_levels(key, extent, cuts, -0.22, 0.18) if cuts else 1.0
    entries = jax.random.normal(key, extent, jnp.float32) * spread * gain
    return jnp.minimum(jnp.maximum(entries, -most), most).astype(kind)


def setup_inputs(seed: int = 0) -> dict:
    splits = jax.random.split(jax.random.key(seed), 3)
    start_state = draw_start_state(jax.random.fold_in(splits[2], 71), 0)
    node_offset = gaussian(splits[1], (TIME_NODES, VARIABLES, BASIS, BASIS, BASIS, NXE, PLANE), 0.15, 0.6, ((0, 4), (5, 8)), jnp.float32)
    return dict(start_state=start_state, node_offset=node_offset)


gamma_gas = 1.4
step_length = 0.01
inverse_weight = 6.0
highest = lax.Precision.HIGHEST
derivative_forms = ('ia,vabcxyz->vibcxyz', 'ib,vabcxyz->vaicxyz', 'ic,vabcxyz->vabixyz')

def lobatto_derivative():
    points = np.array([-1.0, -math.sqrt(0.2), math.sqrt(0.2), 1.0])
    barycentric = np.ones(4)
    for i in range(4):
        for k in range(4):
            if k != i:
                barycentric[i] = barycentric[i] / (points[i] - points[k])
    derivative = np.zeros((4, 4))
    for i in range(4):
        for j in range(4):
            if i != j:
                derivative[i, j] = barycentric[j] / barycentric[i] / (points[i] - points[j])
        derivative[i, i] = -np.sum(derivative[i])
    return derivative

def collocation_matrix():
    near_root = math.sqrt(3.0 / 7 - 2.0 / 7 * math.sqrt(1.2))
    far_root = math.sqrt(3.0 / 7 + 2.0 / 7 * math.sqrt(1.2))
    time_nodes = [(1.0 + value) / 2 for value in (-far_root, -near_root, near_root, far_root)]
    quad_table = np.zeros((4, 4))
    for j in range(4):
        coeffs = [1.0]
        for k in range(4):
            if k != j:
                scale = 1.0 / (time_nodes[j] - time_nodes[k])
                widened = [0.0] * (len(coeffs) + 1)
                for power in range(len(coeffs)):
                    widened[power + 1] = widened[power + 1] + coeffs[power] * scale
                    widened[power] = widened[power] - time_nodes[k] * coeffs[power] * scale
                coeffs = widened
        for m in range(4):
            total = 0.0
            for power in range(len(coeffs)):
                total = total + coeffs[power] * time_nodes[m] ** (power + 1) / (power + 1)
            quad_table[m, j] = total
    return quad_table

def physical_flux(state, direction):
    density = state[0]
    momenta = state[1:4]
    energy = state[4]
    velocity = momenta / density
    pressure = (gamma_gas - 1.0) * (energy - 0.5 * lax.optimization_barrier(jnp.sum(momenta * velocity, axis=0)))
    normal_speed = velocity[direction]
    columns = [momenta[direction]]
    for component in range(3):
        entry = momenta[component] * normal_speed
        if component == direction:
            entry = entry + pressure
        columns.append(entry)
    columns.append((energy + pressure) * normal_speed)
    return (jnp.stack(columns), jnp.abs(normal_speed) + jnp.sqrt(gamma_gas * pressure / density))

def face_flux(left_state, right_state, direction):
    left_flux, left_wave = physical_flux(left_state, direction)
    right_flux, right_wave = physical_flux(right_state, direction)
    wave_speed = jnp.maximum(left_wave, right_wave)
    return 0.5 * (left_flux + right_flux) - 0.5 * wave_speed * (right_state - left_state)

def edge_slice(array, dim, first):
    return lax.slice_in_dim(array, first, first + 1, axis=dim)

def with_surface(first_term, last_term, dim):
    filler = jnp.zeros_like(first_term)
    return jnp.concatenate([first_term, filler, filler, last_term], axis=dim)

def element_rate(state):
    cube = state.reshape(state.shape[:5] + (EY, EZ))
    derivative = jnp.asarray(lobatto_derivative(), jnp.float32)
    total_rate = jnp.zeros_like(cube)
    for direction in range(3):
        flux, wave_unused = physical_flux(cube, direction)
        total_rate = total_rate - jnp.einsum(derivative_forms[direction], derivative, flux, precision=highest)
        node_dim = 1 + direction
        elem_dim = 4 + direction
        own_first = edge_slice(cube, node_dim, 0)
        own_last = edge_slice(cube, node_dim, 3)
        right_faces = face_flux(own_last, jnp.roll(own_first, -1, axis=elem_dim), direction)
        left_faces = jnp.roll(right_faces, 1, axis=elem_dim)
        flux_first = edge_slice(flux, node_dim, 0)
        flux_last = edge_slice(flux, node_dim, 3)
        total_rate = total_rate + inverse_weight * with_surface(left_faces - flux_first, flux_last - right_faces, node_dim)
    return total_rate.reshape(state.shape)

def reference(start_state, node_offset):
    quad_table = jnp.asarray(collocation_matrix(), jnp.float32)
    states = [start_state + node_offset[position] for position in range(4)]
    results = []
    for iteration in range(ITERS):
        rates = [element_rate(current) for current in states]
        results = []
        for target in range(4):
            running = quad_table[target, 0] * rates[0]
            for source in range(1, 4):
                running = running + quad_table[target, source] * rates[source]
            results.append(step_length * running)
        states = [start_state + change for change in results]
    return jnp.stack(results)
```

```python
import functools
import math

import jax
import jax.numpy as jnp
import numpy as np
from jax import lax
from jax.experimental import pallas as pl
from jax.experimental.pallas import tpu as pltpu
from jax.sharding import PartitionSpec as P

EZ = 80
QUARTER = 320
TILES = 10
ITERS = 2
gamma_gas = 1.4
step_length = 0.01
VMEM_LIMIT = 48 * 1024 * 1024


def lobatto_derivative():
    points = np.array([-1.0, -math.sqrt(0.2), math.sqrt(0.2), 1.0])
    barycentric = np.ones(4)
    for i in range(4):
        for k in range(4):
            if k != i:
                barycentric[i] = barycentric[i] / (points[i] - points[k])
    derivative = np.zeros((4, 4))
    for i in range(4):
        for j in range(4):
            if i != j:
                derivative[i, j] = barycentric[j] / barycentric[i] / (points[i] - points[j])
        derivative[i, i] = -np.sum(derivative[i])
    return derivative


def collocation_matrix():
    near_root = math.sqrt(3.0 / 7 - 2.0 / 7 * math.sqrt(1.2))
    far_root = math.sqrt(3.0 / 7 + 2.0 / 7 * math.sqrt(1.2))
    time_nodes = [(1.0 + value) / 2 for value in (-far_root, -near_root, near_root, far_root)]
    quad_table = np.zeros((4, 4))
    for j in range(4):
        coeffs = [1.0]
        for k in range(4):
            if k != j:
                scale = 1.0 / (time_nodes[j] - time_nodes[k])
                widened = [0.0] * (len(coeffs) + 1)
                for power in range(len(coeffs)):
                    widened[power + 1] = widened[power + 1] + coeffs[power] * scale
                    widened[power] = widened[power] - time_nodes[k] * coeffs[power] * scale
                coeffs = widened
        for m in range(4):
            total = 0.0
            for power in range(len(coeffs)):
                total = total + coeffs[power] * time_nodes[m] ** (power + 1) / (power + 1)
            quad_table[m, j] = total
    return quad_table


DERIV = np.float32(lobatto_derivative())
QUAD = np.float32(step_length * collocation_matrix())
VREG = (8, 128)


def lanes():
    return lax.broadcasted_iota(jnp.int32, VREG, 1)


def sublanes():
    return lax.broadcasted_iota(jnp.int32, VREG, 0)


def lane_roll(tiles, shift):
    count = len(tiles)
    whole, rest = divmod(shift % (128 * count), 128)
    if rest == 0:
        return [tiles[(t - whole) % count] for t in range(count)]
    rotated = [pltpu.roll(tile, rest, 1) for tile in tiles]
    lane = lanes()
    return [
        jnp.where(lane < rest, rotated[(t - whole - 1) % count], rotated[(t - whole) % count])
        for t in range(count)
    ]


def primitive(state):
    rho, m1, m2, m3, energy = state
    inverse = 1.0 / rho
    v1, v2, v3 = m1 * inverse, m2 * inverse, m3 * inverse
    pressure = (gamma_gas - 1.0) * (energy - 0.5 * (m1 * v1 + m2 * v2 + m3 * v3))
    return inverse, (v1, v2, v3), pressure


def flux_entry(state, velocity, pressure, variable, direction):
    speed = velocity[direction]
    if variable == 0:
        return state[1 + direction]
    if variable == 4:
        return (state[4] + pressure) * speed
    entry = state[variable] * speed
    if variable - 1 == direction:
        entry = entry + pressure
    return entry


def wave(inverse, velocity, pressure, direction):
    square = gamma_gas * pressure * inverse
    return jnp.abs(velocity[direction]) + square * lax.rsqrt(square)


def face_terms(own, other, direction, sign):
    own_inv, own_v, own_p = primitive(own)
    oth_inv, oth_v, oth_p = primitive(other)
    speed = 3.0 * jnp.maximum(
        wave(own_inv, own_v, own_p, direction), wave(oth_inv, oth_v, oth_p, direction)
    )
    weight = 3.0 * sign
    terms = []
    for variable in range(5):
        jump = other[variable] - own[variable]
        flux_jump = flux_entry(own, own_v, own_p, variable, direction) - flux_entry(
            other, oth_v, oth_p, variable, direction
        )
        terms.append(speed * jump + weight * flux_jump)
    return terms


def z_partners(u_ref, pz_ref):
    lane = lanes()
    slot = sublanes() % 4

    def one_variable(v, carry):
        for pair in range(2):
            for r in range(2):
                rows = slice(8 * r, 8 * r + 8)
                mixed = []
                for t in range(TILES):
                    even = u_ref[t, v * 4 + 2 * pair, rows, :]
                    odd = u_ref[t, v * 4 + 2 * pair + 1, rows, :]
                    low = jnp.where(slot == 0, pltpu.roll(even, 5, 0), pltpu.roll(odd, 6, 0))
                    high = jnp.where(slot == 3, pltpu.roll(even, 3, 0), pltpu.roll(odd, 2, 0))
                    mixed.append(jnp.where(slot < 2, low, high))
                before = lane_roll(mixed, 1)
                before_wrap = lane_roll(mixed, -(EZ - 1))
                after = lane_roll(mixed, -1)
                after_wrap = lane_roll(mixed, EZ - 1)
                for t in range(TILES):
                    column = (lane + 128 * t) % EZ
                    low = jnp.where(column == 0, before_wrap[t], before[t])
                    high = jnp.where(column == EZ - 1, after_wrap[t], after[t])
                    pz_ref[t, v * 2 + pair, rows, :] = jnp.where(slot < 2, low, high)
        return carry

    lax.fori_loop(0, 5, one_variable, 0)


def y_partners(u_ref, py_ref, below_ref=None, above_ref=None):
    lane = lanes()
    lower = sublanes() < 4

    def one_block(q, carry):
        swapped = []
        for t in range(TILES):
            trace = jnp.where(lower, u_ref[t, q, 0:8, :], u_ref[t, q, 8:16, :])
            swapped.append(pltpu.roll(trace, 4, 0))
        before = lane_roll(swapped, EZ)
        after = lane_roll(swapped, -EZ)
        if below_ref is not None:
            for m in range(4):
                half, odd = m % 2, m // 2
                got = below_ref[q * 2 + m // 2]
                if half == 1:
                    got = pltpu.roll(got, 4, 0)
                got = pltpu.roll(got, 16 + 64 * half, 1)
                base = 5 * (m // 2)
                if half == 0:
                    before[base] = jnp.where(lane < 80, got, before[base])
                else:
                    before[base + 2] = jnp.where(lane >= 64, got, before[base + 2])
                    before[base + 3] = jnp.where(lane < 16, got, before[base + 3])
                got = above_ref[q * 2 + m // 2]
                if half == 0:
                    got = pltpu.roll(pltpu.roll(got, 4, 0), 112, 1)
                    after[base + 1] = jnp.where(lane >= 112, got, after[base + 1])
                    after[base + 2] = jnp.where(lane < 64, got, after[base + 2])
                else:
                    got = pltpu.roll(got, 48, 1)
                    after[base + 4] = jnp.where(lane >= 48, got, after[base + 4])
        for t in range(TILES):
            py_ref[t, q] = jnp.where(lower, before[t], after[t])
        return carry

    lax.fori_loop(0, 20, one_block, 0)


def load_state(u_ref, t, a, rows):
    return [u_ref[t, v * 4 + a, rows, :] for v in range(5)]


def z_face_terms(u_ref, pz_ref, t):
    slot = sublanes() % 4
    sign = jnp.where(slot < 2, -1.0, 1.0).astype(jnp.float32)
    result = [[[None, None] for _ in range(4)] for _ in range(5)]
    for pair in range(2):
        for r in range(2):
            rows = slice(8 * r, 8 * r + 8)
            own, other = [], []
            for v in range(5):
                even = u_ref[t, v * 4 + 2 * pair, rows, :]
                odd = u_ref[t, v * 4 + 2 * pair + 1, rows, :]
                inner = jnp.where(slot == 1, pltpu.roll(odd, 1, 0), pltpu.roll(odd, 7, 0))
                own.append(jnp.where((slot == 0) | (slot == 3), even, inner))
                other.append(pz_ref[t, v * 2 + pair, rows, :])
            terms = face_terms(own, other, 2, sign)
            for v in range(5):
                term = terms[v]
                outer = (slot == 0) | (slot == 3)
                result[v][2 * pair][r] = jnp.where(outer, term, 0.0)
                moved = jnp.where(slot == 0, pltpu.roll(term, 7, 0), pltpu.roll(term, 1, 0))
                result[v][2 * pair + 1][r] = jnp.where(outer, moved, 0.0)
    return result


def sublane_column(values):
    row = sublanes()
    block = jnp.full(VREG, float(values[0]), jnp.float32)
    for s in range(1, 8):
        block = jnp.where(row == s, jnp.float32(float(values[s])), block)
    return block


def volume_tile(u_ref, pz_ref, r_ref, coef_ref, t):
    face = z_face_terms(u_ref, pz_ref, t)
    slot = sublanes() % 4
    states = [[load_state(u_ref, t, a, slice(8 * r, 8 * r + 8)) for r in range(2)] for a in range(4)]
    prims = [[primitive(states[a][r]) for r in range(2)] for a in range(4)]
    for v in range(5):
        total = face[v]
        for r in range(2):
            column = [flux_entry(states[a][r], prims[a][r][1], prims[a][r][2], v, 0) for a in range(4)]
            for a in range(4):
                for other in range(4):
                    total[a][r] = total[a][r] - float(DERIV[a, other]) * column[other]
        for a in range(4):
            first = flux_entry(states[a][0], prims[a][0][1], prims[a][0][2], v, 1)
            second = flux_entry(states[a][1], prims[a][1][1], prims[a][1][2], v, 1)
            parts = [first, pltpu.roll(first, 4, 0), second, pltpu.roll(second, 4, 0)]
            for r in range(2):
                for k in range(4):
                    total[a][r] = total[a][r] - coef_ref[4 * r + k] * parts[k]
            for r in range(2):
                flux = flux_entry(states[a][r], prims[a][r][1], prims[a][r][2], v, 2)
                across = pltpu.roll(flux, 4, 0)
                acc = total[a][r] - coef_ref[8] * flux
                for shift in range(1, 4):
                    mixed = pltpu.roll(jnp.where(slot < 4 - shift, flux, across), shift, 0)
                    acc = acc - coef_ref[8 + shift] * mixed
                r_ref[t, v * 4 + a, slice(8 * r, 8 * r + 8), :] = acc


def coefficient_table():
    table = np.zeros((12, 8, 128), np.float32)
    for s in range(8):
        group, c = divmod(s, 4)
        for r in range(2):
            b = 2 * r + group
            for k in range(4):
                source = 2 * (k // 2) + (group if k % 2 == 0 else 1 - group)
                table[4 * r + k, s, :] = DERIV[b, source]
        for shift in range(4):
            table[8 + shift, s, :] = DERIV[c, (c - shift) % 4]
    return table


def y_face_tile(u_ref, py_ref, r_ref, t):
    lower = sublanes() < 4
    sign = jnp.where(lower, -1.0, 1.0).astype(jnp.float32)
    for a in range(4):
        own = [jnp.where(lower, u_ref[t, v * 4 + a, 0:8, :], u_ref[t, v * 4 + a, 8:16, :]) for v in range(5)]
        other = [py_ref[t, v * 4 + a] for v in range(5)]
        terms = face_terms(own, other, 1, sign)
        for v in range(5):
            r_ref[t, v * 4 + a, 0:8, :] += jnp.where(lower, terms[v], 0.0)
            r_ref[t, v * 4 + a, 8:16, :] += jnp.where(lower, 0.0, terms[v])


def x_face_tile(u_ref, left_ref, right_ref, r_ref, t):
    for r in range(2):
        rows = slice(8 * r, 8 * r + 8)
        for a, ref, sign in ((0, left_ref, -1.0), (3, right_ref, 1.0)):
            own = load_state(u_ref, t, a, rows)
            other = [ref[t, v, rows, :] for v in range(5)]
            terms = face_terms(own, other, 0, sign)
            for v in range(5):
                r_ref[t, v * 4 + a, rows, :] += terms[v]


def pack_pair(tiles):
    lane = lanes()
    low = lane < 64
    flip = [[pltpu.roll(half, 64, 1) for half in tile] for tile in tiles]
    first = [
        tiles[0][0],
        tiles[1][0],
        tiles[0][1],
        tiles[1][1],
        jnp.where(low, tiles[2][0], flip[2][1]),
    ]
    second = [
        jnp.where(low, flip[2][0], flip[3][0]),
        jnp.where(low, flip[3][0], flip[4][0]),
        jnp.where(low, flip[2][1], flip[3][1]),
        jnp.where(low, flip[3][1], flip[4][1]),
        jnp.where(low, flip[4][0], tiles[4][1]),
    ]
    return first, second


def unpack_pair(first, second):
    low = lanes() < 64
    flip_first = pltpu.roll(first[4], 64, 1)
    flip = [pltpu.roll(block, 64, 1) for block in second]
    return [
        [first[0], first[2]],
        [first[1], first[3]],
        [jnp.where(low, first[4], flip[0]), jnp.where(low, flip_first, flip[2])],
        [jnp.where(low, flip[0], flip[1]), jnp.where(low, flip[2], flip[3])],
        [jnp.where(low, flip[1], flip[4]), jnp.where(low, flip[3], second[4])],
    ]


def load_tiles(ref, q, base):
    return [[ref[base + i, q, 0:8, :], ref[base + i, q, 8:16, :]] for i in range(5)]


def start_kernel(rank_ref, start_ref, offset_ref, u_ref, last_ref, first_ref, piece_ref):
    rank = rank_ref[0]
    base = (5 * rank) // 2
    shift = (128 - 64 * (rank % 2)) % 128
    lane = lanes()
    keep = lane < 128 - 64 * (rank % 2)
    low = lane < 64

    def rows(q, r, t):
        return pl.ds((q * 16 + 8 * r) * 10 + t, 8, stride=10)

    def one_block(q, carry):
        a = q % 4
        for t in range(TILES):
            for r in range(2):
                block = start_ref[rows(q, r, t), :] + offset_ref[rows(q, r, t), :]
                u_ref[t, q, 8 * r : 8 * r + 8, :] = block
        turned = [
            [pltpu.roll(start_ref[rows(q, r, base + i), :], shift, 1) for r in range(2)] for i in range(3)
        ]
        for r in range(2):
            piece_ref[q, 2 * r] = jnp.where(keep, turned[0][r], turned[1][r])
            piece_ref[q, 2 * r + 1] = jnp.where(keep, turned[1][r], turned[2][r])
        piece_ref[q, 4] = jnp.where(low, turned[2][0], pltpu.roll(turned[2][1], 64, 1))
        return carry

    lax.fori_loop(0, 20, one_block, 0)
    for v in range(5):
        first_ref[:, v] = u_ref[:, v * 4]
        last_ref[:, v] = u_ref[:, v * 4 + 3]


def full_inner_kernel(coef_ref, u_ref, r_ref, pz_ref, py_ref):
    z_partners(u_ref, pz_ref)
    y_partners(u_ref, py_ref)

    def one_tile(t, carry):
        volume_tile(u_ref, pz_ref, r_ref, coef_ref, t)
        y_face_tile(u_ref, py_ref, r_ref, t)
        return carry

    lax.fori_loop(0, TILES, one_tile, 0)


def full_outer_kernel(u_ref, inner_ref, left_ref, right_ref, piece_ref, r_ref):
    def one_tile(t, carry):
        r_ref[t] = inner_ref[t]
        x_face_tile(u_ref, left_ref, right_ref, r_ref, t)
        return carry

    lax.fori_loop(0, TILES, one_tile, 0)

    def one_block(q, carry):
        for pair in range(2):
            packed = pack_pair(load_tiles(r_ref, q, 5 * pair))
            for half in range(2):
                for i in range(5):
                    piece_ref[2 * pair + half, q, i] = packed[half][i]
        return carry

    lax.fori_loop(0, 20, one_block, 0)


def guess_kernel(rates_ref, start_ref, u_ref, last_ref, first_ref, up_ref, down_ref):
    lower = sublanes() < 4
    low = lanes() < 64

    def one_block(q, carry):
        pieces = []
        for m in range(4):
            blocks = []
            for i in range(5):
                total = start_ref[q, i]
                for j in range(4):
                    total = total + float(QUAD[m, j]) * rates_ref[j, q, i]
                blocks.append(total)
            pieces.append(blocks)
        for pair in range(2):
            even, odd = pieces[2 * pair], pieces[2 * pair + 1]
            tiles = unpack_pair(even, odd)
            for i in range(5):
                for r in range(2):
                    u_ref[5 * pair + i, q, 8 * r : 8 * r + 8, :] = tiles[i][r]
            down_ref[q * 2 + pair] = jnp.where(lower, even[0], pltpu.roll(odd[0], 4, 0))
            tops = [jnp.where(low, pltpu.roll(piece[4], 64, 1), piece[3]) for piece in (even, odd)]
            up_ref[q * 2 + pair] = jnp.where(lower, pltpu.roll(tops[0], 4, 0), tops[1])
        return carry

    lax.fori_loop(0, 20, one_block, 0)
    for v in range(5):
        first_ref[:, v] = u_ref[:, v * 4]
        last_ref[:, v] = u_ref[:, v * 4 + 3]


def quarter_inner_kernel(coef_ref, u_ref, r_ref, pz_ref):
    z_partners(u_ref, pz_ref)

    def one_tile(t, carry):
        volume_tile(u_ref, pz_ref, r_ref, coef_ref, t)
        return carry

    lax.fori_loop(0, TILES, one_tile, 0)


def quarter_outer_kernel(u_ref, inner_ref, left_ref, right_ref, below_ref, above_ref, piece_ref, r_ref, py_ref):
    y_partners(u_ref, py_ref, below_ref, above_ref)

    def one_tile(t, carry):
        r_ref[t] = inner_ref[t]
        y_face_tile(u_ref, py_ref, r_ref, t)
        x_face_tile(u_ref, left_ref, right_ref, r_ref, t)
        return carry

    lax.fori_loop(0, TILES, one_tile, 0)

    def one_block(q, carry):
        pieces = []
        for pair in range(2):
            pieces.extend(pack_pair(load_tiles(r_ref, q, 5 * pair)))
        for m in range(4):
            for i in range(5):
                total = float(QUAD[m, 0]) * pieces[0][i]
                for j in range(1, 4):
                    total = total + float(QUAD[m, j]) * pieces[j][i]
                piece_ref[m, q, i] = total
        return carry

    lax.fori_loop(0, 20, one_block, 0)


def finish_kernel(piece_ref, out_ref):
    def one_block(q, carry):
        for pair in range(2):
            pieces = [[piece_ref[2 * pair + half, q, i] for i in range(5)] for half in range(2)]
            tiles = unpack_pair(*pieces)
            for i in range(5):
                for r in range(2):
                    out_ref[pl.ds((q * 16 + 8 * r) * 10 + 5 * pair + i, 8, stride=10), :] = tiles[i][r]
        return carry

    lax.fori_loop(0, 20, one_block, 0)


def f32(*shape):
    return jax.ShapeDtypeStruct(shape, jnp.float32)


def vmem(count):
    return [pl.BlockSpec(memory_space=pltpu.VMEM)] * count


def call(kernel, outs, args, scratch=(), scalar=None, flops=0):
    specs = vmem(len(args))
    if scalar is not None:
        specs = [pl.BlockSpec(memory_space=pltpu.SMEM)] + specs
        args = (scalar,) + tuple(args)
    single = not isinstance(outs, (list, tuple))
    count = 1 if single else len(outs)
    moved = sum(4 * math.prod(a.shape) for a in args)
    moved += sum(4 * math.prod(o.shape) for o in ([outs] if single else outs))
    return pl.pallas_call(
        kernel,
        out_shape=outs,
        in_specs=specs,
        out_specs=vmem(1)[0] if single else vmem(count),
        scratch_shapes=[pltpu.VMEM(shape, jnp.float32) for shape in scratch],
        compiler_params=pltpu.CompilerParams(vmem_limit_bytes=VMEM_LIMIT),
        cost_estimate=pl.CostEstimate(flops=flops, bytes_accessed=moved, transcendentals=0),
    )(*args)


def shifted(block, axis, distance):
    count = lax.axis_size(axis)
    return lax.ppermute(block, axis, [((i - distance) % count, i) for i in range(count)])


STATE = (TILES, 20, 16, 128)
TRACE = (TILES, 5, 16, 128)
PIECE = (20, 5, 8, 128)
EDGE = (40, 8, 128)


def body(start_state, node_offset):
    flat = (3200, 128)
    start_flat = start_state.reshape(flat)
    offset_flat = node_offset.reshape(flat)
    rank = lax.axis_index("node").astype(jnp.int32).reshape(1)
    coef = jnp.asarray(coefficient_table())

    guess, last, first, start_piece = call(
        start_kernel,
        [f32(*STATE), f32(*TRACE), f32(*TRACE), f32(*PIECE)],
        (start_flat, offset_flat),
        scalar=rank,
    )
    left = shifted(last, "space", 1)
    right = shifted(first, "space", -1)
    inner = call(
        full_inner_kernel,
        f32(*STATE),
        (coef, guess),
        scratch=[(TILES, 10, 16, 128), (TILES, 20, 8, 128)],
        flops=30_000_000,
    )
    pieces = call(
        full_outer_kernel, f32(4, *PIECE), (guess, inner, left, right), scratch=[STATE]
    )
    rates = lax.all_to_all(pieces, "node", 0, 0, tiled=True)
    guess, last, first, up, down = call(
        guess_kernel,
        [f32(*STATE), f32(*TRACE), f32(*TRACE), f32(*EDGE), f32(*EDGE)],
        (rates, start_piece),
    )
    left = shifted(last, "space", 1)
    right = shifted(first, "space", -1)
    below = shifted(up, "node", 1)
    above = shifted(down, "node", -1)
    inner = call(
        quarter_inner_kernel,
        f32(*STATE),
        (coef, guess),
        scratch=[(TILES, 10, 16, 128)],
        flops=30_000_000,
    )
    pieces = call(
        quarter_outer_kernel,
        f32(4, *PIECE),
        (guess, inner, left, right, below, above),
        scratch=[STATE, (TILES, 20, 8, 128)],
    )
    pieces = lax.all_to_all(pieces, "node", 0, 0, tiled=True)
    result = call(finish_kernel, f32(*flat), (pieces,))
    return result.reshape(node_offset.shape)


def solution(mesh):
    return jax.shard_map(
        body,
        mesh=mesh,
        in_specs=(
            P(None, None, None, None, "space", None),
            P("node", None, None, None, None, "space", None),
        ),
        out_specs=P("node", None, None, None, None, "space", None),
        check_vma=False,
    )
```

```python
import functools
import math

import jax
import jax.numpy as jnp
import numpy as np
from jax import lax
from jax.experimental import pallas as pl
from jax.experimental.pallas import tpu as pltpu
from jax.sharding import PartitionSpec as P

EZ = 80
QUARTER = 320
TILES = 10
ITERS = 2
gamma_gas = 1.4
step_length = 0.01
VMEM_LIMIT = 48 * 1024 * 1024


def lobatto_derivative():
    points = np.array([-1.0, -math.sqrt(0.2), math.sqrt(0.2), 1.0])
    barycentric = np.ones(4)
    for i in range(4):
        for k in range(4):
            if k != i:
                barycentric[i] = barycentric[i] / (points[i] - points[k])
    derivative = np.zeros((4, 4))
    for i in range(4):
        for j in range(4):
            if i != j:
                derivative[i, j] = barycentric[j] / barycentric[i] / (points[i] - points[j])
        derivative[i, i] = -np.sum(derivative[i])
    return derivative


def collocation_matrix():
    near_root = math.sqrt(3.0 / 7 - 2.0 / 7 * math.sqrt(1.2))
    far_root = math.sqrt(3.0 / 7 + 2.0 / 7 * math.sqrt(1.2))
    time_nodes = [(1.0 + value) / 2 for value in (-far_root, -near_root, near_root, far_root)]
    quad_table = np.zeros((4, 4))
    for j in range(4):
        coeffs = [1.0]
        for k in range(4):
            if k != j:
                scale = 1.0 / (time_nodes[j] - time_nodes[k])
                widened = [0.0] * (len(coeffs) + 1)
                for power in range(len(coeffs)):
                    widened[power + 1] = widened[power + 1] + coeffs[power] * scale
                    widened[power] = widened[power] - time_nodes[k] * coeffs[power] * scale
                coeffs = widened
        for m in range(4):
            total = 0.0
            for power in range(len(coeffs)):
                total = total + coeffs[power] * time_nodes[m] ** (power + 1) / (power + 1)
            quad_table[m, j] = total
    return quad_table


DERIV = np.float32(lobatto_derivative())
QUAD = np.float32(step_length * collocation_matrix())
VREG = (8, 128)


def lanes():
    return lax.broadcasted_iota(jnp.int32, VREG, 1)


def sublanes():
    return lax.broadcasted_iota(jnp.int32, VREG, 0)


def lane_roll(tiles, shift):
    count = len(tiles)
    whole, rest = divmod(shift % (128 * count), 128)
    if rest == 0:
        return [tiles[(t - whole) % count] for t in range(count)]
    rotated = [pltpu.roll(tile, rest, 1) for tile in tiles]
    lane = lanes()
    return [
        jnp.where(lane < rest, rotated[(t - whole - 1) % count], rotated[(t - whole) % count])
        for t in range(count)
    ]


def primitive(state):
    rho, m1, m2, m3, energy = state
    inverse = 1.0 / rho
    v1, v2, v3 = m1 * inverse, m2 * inverse, m3 * inverse
    pressure = (gamma_gas - 1.0) * (energy - 0.5 * (m1 * v1 + m2 * v2 + m3 * v3))
    return inverse, (v1, v2, v3), pressure


def flux_entry(state, velocity, pressure, variable, direction):
    speed = velocity[direction]
    if variable == 0:
        return state[1 + direction]
    if variable == 4:
        return (state[4] + pressure) * speed
    entry = state[variable] * speed
    if variable - 1 == direction:
        entry = entry + pressure
    return entry


def wave(inverse, velocity, pressure, direction):
    square = gamma_gas * pressure * inverse
    return jnp.abs(velocity[direction]) + square * lax.rsqrt(square)


def face_terms(own, other, direction, sign):
    own_inv, own_v, own_p = primitive(own)
    oth_inv, oth_v, oth_p = primitive(other)
    speed = 3.0 * jnp.maximum(
        wave(own_inv, own_v, own_p, direction), wave(oth_inv, oth_v, oth_p, direction)
    )
    weight = 3.0 * sign
    terms = []
    for variable in range(5):
        jump = other[variable] - own[variable]
        flux_jump = flux_entry(own, own_v, own_p, variable, direction) - flux_entry(
            other, oth_v, oth_p, variable, direction
        )
        terms.append(speed * jump + weight * flux_jump)
    return terms


def z_partners(pair, pz_ref):
    lane = lanes()
    slot = sublanes() % 4
    even_ref, odd_ref = pair

    def one_variable(v, carry):
        for r in range(2):
            rows = slice(8 * r, 8 * r + 8)
            mixed = []
            for t in range(TILES):
                even = even_ref[t, v, rows, :]
                odd = odd_ref[t, v, rows, :]
                low = jnp.where(slot == 0, pltpu.roll(even, 5, 0), pltpu.roll(odd, 6, 0))
                high = jnp.where(slot == 3, pltpu.roll(even, 3, 0), pltpu.roll(odd, 2, 0))
                mixed.append(jnp.where(slot < 2, low, high))
            before = lane_roll(mixed, 1)
            before_wrap = lane_roll(mixed, -(EZ - 1))
            after = lane_roll(mixed, -1)
            after_wrap = lane_roll(mixed, EZ - 1)
            for t in range(TILES):
                column = (lane + 128 * t) % EZ
                low = jnp.where(column == 0, before_wrap[t], before[t])
                high = jnp.where(column == EZ - 1, after_wrap[t], after[t])
                pz_ref[t, v, rows, :] = jnp.where(slot < 2, low, high)
        return carry

    lax.fori_loop(0, 5, one_variable, 0)


def y_partners(u_ref, py_ref, halo_ref=None):
    lane = lanes()
    lower = sublanes() < 4

    def one_variable(v, carry):
        swapped = []
        for t in range(TILES):
            trace = jnp.where(lower, u_ref[t, v, 0:8, :], u_ref[t, v, 8:16, :])
            swapped.append(pltpu.roll(trace, 4, 0))
        before = lane_roll(swapped, EZ)
        after = lane_roll(swapped, -EZ)
        if halo_ref is not None:
            for m in range(4):
                base = 5 * (m // 2)
                got = pltpu.roll(halo_ref[m, v], 4, 0)
                if m % 2 == 0:
                    before[base] = jnp.where(lane < 80, got, before[base])
                    moved = pltpu.roll(got, 112, 1)
                    after[base + 1] = jnp.where(lane >= 112, moved, after[base + 1])
                    after[base + 2] = jnp.where(lane < 64, moved, after[base + 2])
                else:
                    moved = pltpu.roll(got, 64, 1)
                    before[base + 2] = jnp.where(lane >= 64, moved, before[base + 2])
                    before[base + 3] = jnp.where(lane < 16, moved, before[base + 3])
                    moved = pltpu.roll(got, 48, 1)
                    after[base + 4] = jnp.where(lane >= 48, moved, after[base + 4])
        for t in range(TILES):
            py_ref[t, v] = jnp.where(lower, before[t], after[t])
        return carry

    lax.fori_loop(0, 5, one_variable, 0)


def load_state(u_ref, t, rows):
    return [u_ref[t, v, rows, :] for v in range(5)]


def z_face_terms(pair, pz_ref, t):
    slot = sublanes() % 4
    outer = (slot == 0) | (slot == 3)
    sign = jnp.where(slot < 2, -1.0, 1.0).astype(jnp.float32)
    result = [[[None, None] for _ in range(2)] for _ in range(5)]
    for r in range(2):
        rows = slice(8 * r, 8 * r + 8)
        own, other = [], []
        for v in range(5):
            even = pair[0][t, v, rows, :]
            odd = pair[1][t, v, rows, :]
            inner = jnp.where(slot == 1, pltpu.roll(odd, 1, 0), pltpu.roll(odd, 7, 0))
            own.append(jnp.where(outer, even, inner))
            other.append(pz_ref[t, v, rows, :])
        terms = face_terms(own, other, 2, sign)
        for v in range(5):
            term = terms[v]
            result[v][0][r] = jnp.where(outer, term, 0.0)
            moved = jnp.where(slot == 0, pltpu.roll(term, 7, 0), pltpu.roll(term, 1, 0))
            result[v][1][r] = jnp.where(outer, moved, 0.0)
    return result


def volume_tile(t, states, targets, coef_ref, start, emit):
    slot = sublanes() % 4
    state, prim = {}, {}
    for a, ref in states.items():
        for r in range(2):
            state[a, r] = load_state(ref, t, slice(8 * r, 8 * r + 8))
            prim[a, r] = primitive(state[a, r])

    def flux(a, r, v, direction):
        return flux_entry(state[a, r], prim[a, r][1], prim[a, r][2], v, direction)

    for v in range(5):
        total = {}
        for r in range(2):
            column = {a: flux(a, r, v, 0) for a in states}
            for a in targets:
                value = start(v, a, r)
                for other in states:
                    term = float(-DERIV[a, other]) * column[other]
                    value = term if value is None else value + term
                total[a, r] = value
        for a, whole in targets.items():
            if whole:
                first, second = flux(a, 0, v, 1), flux(a, 1, v, 1)
                parts = [first, pltpu.roll(first, 4, 0), second, pltpu.roll(second, 4, 0)]
                for r in range(2):
                    for k in range(4):
                        total[a, r] = total[a, r] - coef_ref[4 * r + k] * parts[k]
            for r in range(2):
                acc = total[a, r]
                if whole:
                    along = flux(a, r, v, 2)
                    across = pltpu.roll(along, 4, 0)
                    acc = acc - coef_ref[8] * along
                    for shift in range(1, 4):
                        mixed = pltpu.roll(jnp.where(slot < 4 - shift, along, across), shift, 0)
                        acc = acc - coef_ref[8 + shift] * mixed
                emit(v, a, r, acc)


def coefficient_table():
    table = np.zeros((12, 8, 128), np.float32)
    for s in range(8):
        group, c = divmod(s, 4)
        for r in range(2):
            b = 2 * r + group
            for k in range(4):
                source = 2 * (k // 2) + (group if k % 2 == 0 else 1 - group)
                table[4 * r + k, s, :] = DERIV[b, source]
        for shift in range(4):
            table[8 + shift, s, :] = DERIV[c, (c - shift) % 4]
    return table


def y_face_tile(u_ref, py_ref, r_ref, which, t):
    lower = sublanes() < 4
    sign = jnp.where(lower, -1.0, 1.0).astype(jnp.float32)
    own = [jnp.where(lower, u_ref[t, v, 0:8, :], u_ref[t, v, 8:16, :]) for v in range(5)]
    terms = face_terms(own, [py_ref[t, v] for v in range(5)], 1, sign)
    for v in range(5):
        r_ref[t, v * 2 + which, 0:8, :] += jnp.where(lower, terms[v], 0.0)
        r_ref[t, v * 2 + which, 8:16, :] += jnp.where(lower, 0.0, terms[v])


def x_face_tile(u_ref, other_ref, r_ref, which, t):
    sign = -1.0 if which == 0 else 1.0
    for r in range(2):
        rows = slice(8 * r, 8 * r + 8)
        terms = face_terms(load_state(u_ref, t, rows), load_state(other_ref, t, rows), 0, sign)
        for v in range(5):
            r_ref[t, v * 2 + which, rows, :] += terms[v]


def rates_tile(t, states, pair, sources, pz_ref, py_refs, r_ref, coef_ref, added=None, extra=None):
    targets = {a: True for a in pair}
    refs = [states[a] for a in pair]
    face = z_face_terms(refs, pz_ref, t)

    def start(v, a, r):
        if a not in pair:
            return None
        which = pair.index(a)
        value = face[v][which][r]
        if added is not None:
            value = value + added[t, v * 2 + which, 8 * r : 8 * r + 8, :]
        return value

    def emit(v, a, r, value):
        if a in pair:
            r_ref[t, v * 2 + pair.index(a), 8 * r : 8 * r + 8, :] = value
        else:
            extra[1][t, v * 2 + extra[0].index(a), 8 * r : 8 * r + 8, :] = value

    if extra is not None:
        targets.update({a: False for a in extra[0]})
    volume_tile(t, {a: states[a] for a in sources}, targets, coef_ref, start, emit)
    for which in range(2):
        y_face_tile(refs[which], py_refs[which], r_ref, which, t)


def pack_pair(tiles):
    lane = lanes()
    low = lane < 64
    flip = [[pltpu.roll(half, 64, 1) for half in tile] for tile in tiles]
    first = [
        tiles[0][0],
        tiles[1][0],
        tiles[0][1],
        tiles[1][1],
        jnp.where(low, tiles[2][0], flip[2][1]),
    ]
    second = [
        jnp.where(low, flip[2][0], flip[3][0]),
        jnp.where(low, flip[3][0], flip[4][0]),
        jnp.where(low, flip[2][1], flip[3][1]),
        jnp.where(low, flip[3][1], flip[4][1]),
        jnp.where(low, flip[4][0], tiles[4][1]),
    ]
    return first, second


def unpack_pair(first, second):
    low = lanes() < 64
    flip_first = pltpu.roll(first[4], 64, 1)
    flip = [pltpu.roll(block, 64, 1) for block in second]
    return [
        [first[0], first[2]],
        [first[1], first[3]],
        [jnp.where(low, first[4], flip[0]), jnp.where(low, flip_first, flip[2])],
        [jnp.where(low, flip[0], flip[1]), jnp.where(low, flip[2], flip[3])],
        [jnp.where(low, flip[1], flip[4]), jnp.where(low, flip[3], second[4])],
    ]


PACK_ROWS = 50
HALO_ROWS = 57


def pack_halo_parts(halos):
    lane = lanes()
    packed = [
        jnp.where(lane < 64, halos[2 * v], pltpu.roll(halos[2 * v + 1], 64, 1)) for v in range(5)
    ]
    for first in (0, 8):
        block = None
        for n in range(first, min(first + 8, 10)):
            moved = pltpu.roll(halos[n], (16 * (n - first) + 64) % 128, 1)
            block = moved if block is None else jnp.where(lane < 16 * (n - first), block, moved)
        packed.append(block)
    return packed


def unpack_halo_parts(packed):
    lane = lanes()
    halos = []
    for n in range(10):
        low = packed[n // 2] if n % 2 == 0 else pltpu.roll(packed[n // 2], 64, 1)
        rest = pltpu.roll(packed[5 + n // 8], (64 - 16 * (n % 8)) % 128, 1)
        halos.append(jnp.where(lane < 64, low, rest))
    return halos


def pack_message(load, quarter, out_ref):
    lane = lanes()
    low = lane < 64
    lower = sublanes() < 4
    odd = quarter % 2
    base = (5 * quarter) // 2
    shift = 64 * odd
    keep = lane < 128 - shift
    under = lax.rem(base + 9, 10)
    over = lax.rem(base + 3, 10)
    below_shift = 80 - 64 * odd
    above_shift = 64 - 64 * odd
    halos = []
    for n in range(10):
        top = [load(n, 0, base + i) for i in range(3)]
        bottom = [load(n, 1, base + i) for i in range(3)]
        turned = [[pltpu.roll(x, shift, 1) for x in half] for half in (top, bottom)]
        for r in range(2):
            out_ref[5 * n + 2 * r] = jnp.where(keep, turned[r][0], turned[r][1])
            out_ref[5 * n + 2 * r + 1] = jnp.where(keep, turned[r][1], turned[r][2])
        out_ref[5 * n + 4] = jnp.where(low, turned[0][2], pltpu.roll(bottom[2], above_shift, 1))
        below = jnp.where(
            lane < below_shift,
            pltpu.roll(load(n, 1, under), below_shift, 1),
            pltpu.roll(bottom[0], below_shift, 1),
        )
        above = jnp.where(
            lane < above_shift,
            pltpu.roll(top[2], above_shift, 1),
            pltpu.roll(load(n, 0, over), above_shift, 1),
        )
        halos.append(jnp.where(lower, above, below))
    for i, block in enumerate(pack_halo_parts(halos)):
        out_ref[PACK_ROWS + i] = block


def rate_loader(r_ref):
    return lambda n, r, t: r_ref[t, n, 8 * r : 8 * r + 8, :]


def start_rows(v, a, r, t):
    return pl.ds(((v * 4 + a) * 16 + 8 * r) * 10 + t, 8, stride=10)


def front_kernel(rank_ref, coef_ref, start_hbm, offset_hbm, u0, u1, u2, u3, r_ref, m1, m2, m3, start_ref, offset_ref, pz_ref, py1, py2, sems):
    copies = []
    for v in range(5):
        rows = pl.ds(640 * v, 640)
        pair = [
            pltpu.make_async_copy(start_hbm.at[rows], start_ref.at[rows], sems.at[2 * v]),
            pltpu.make_async_copy(offset_hbm.at[rows], offset_ref.at[rows], sems.at[2 * v + 1]),
        ]
        for copy in pair:
            copy.start()
        copies.append(pair)
    states = {0: u0, 1: u1, 2: u2, 3: u3}
    for v in range(5):
        for copy in copies[v]:
            copy.wait()
        for a in range(4):

            def one_tile(t, carry):
                for r in range(2):
                    rows = start_rows(v, a, r, t)
                    states[a][t, v, 8 * r : 8 * r + 8, :] = start_ref[rows, :] + offset_ref[rows, :]
                return carry

            lax.fori_loop(0, TILES, one_tile, 0, unroll=True)
    z_partners((u1, u2), pz_ref)
    y_partners(u1, py1)
    y_partners(u2, py2)

    def one_tile(t, carry):
        rates_tile(t, states, (1, 2), (0, 1, 2, 3), pz_ref, (py1, py2), r_ref, coef_ref)
        return carry

    lax.fori_loop(0, TILES, one_tile, 0)
    for d, out in ((1, m1), (2, m2), (3, m3)):
        pack_message(rate_loader(r_ref), lax.rem(rank_ref[0] + d, 4), out)


def edge_kernel(rank_ref, coef_ref, u0, u1, u2, u3, left_ref, right_ref, m1, m2, m3, r_ref, pz_ref, py0, py3):
    z_partners((u0, u3), pz_ref)
    y_partners(u0, py0)
    y_partners(u3, py3)
    states = {0: u0, 1: u1, 2: u2, 3: u3}

    def one_tile(t, carry):
        rates_tile(t, states, (0, 3), (0, 1, 2, 3), pz_ref, (py0, py3), r_ref, coef_ref)
        x_face_tile(u0, left_ref, r_ref, 0, t)
        x_face_tile(u3, right_ref, r_ref, 1, t)
        return carry

    lax.fori_loop(0, TILES, one_tile, 0)
    for d, out in ((1, m1), (2, m2), (3, m3)):
        pack_message(rate_loader(r_ref), lax.rem(rank_ref[0] + d, 4), out)


def own_kernel(rank_ref, start_ref, mid_ref, edge_ref, start_mid, start_edge, own_mid, own_edge):
    rank = rank_ref[0]
    for pair, rates, start_out, own_out in (((1, 2), mid_ref, start_mid, own_mid), ((0, 3), edge_ref, start_edge, own_edge)):

        def load(n, r, t):
            return start_ref[start_rows(n // 2, pair[n % 2], r, t), :]

        pack_message(load, rank, start_out)
        pack_message(rate_loader(rates), rank, own_out)


def assemble(rank_ref, table_ref, start_ref, rates, states, halos):
    rank = rank_ref[0]
    weight = [
        [table_ref[m * 4 + lax.rem(rank + 4 - d, 4)] for d in range(4)] for m in range(4)
    ]

    def node_state(m, row):
        total = start_ref[row]
        for d in range(4):
            total = total + weight[m][d] * rates[d][row]
        return total

    def one_variable(v, carry):
        for which in range(2):
            first = 10 * v + 5 * which
            for pair in range(2):
                pieces = [[node_state(2 * pair + half, first + i) for i in range(5)] for half in range(2)]
                tiles = unpack_pair(*pieces)
                for i in range(5):
                    for r in range(2):
                        states[which][5 * pair + i, v, 8 * r : 8 * r + 8, :] = tiles[i][r]
        return carry

    lax.fori_loop(0, 5, one_variable, 0)
    for m in range(4):
        blocks = unpack_halo_parts([node_state(m, PACK_ROWS + i) for i in range(7)])
        for n in range(10):
            halos[n % 2][m, n // 2] = blocks[n]


def send_increments(rank_ref, table_ref, r_ref, outs):
    rank = rank_ref[0]
    weight = [[table_ref[lax.rem(rank + d, 4) * 4 + j] for j in range(4)] for d in range(4)]

    def one_block(n, carry):
        pieces = []
        for pair in range(2):
            tiles = [[r_ref[5 * pair + i, n, 8 * r : 8 * r + 8, :] for r in range(2)] for i in range(5)]
            pieces.extend(pack_pair(tiles))
        for d in range(4):
            for i in range(5):
                total = weight[d][0] * pieces[0][i]
                for j in range(1, 4):
                    total = total + weight[d][j] * pieces[j][i]
                outs[d][5 * n + i] = total
        return carry

    lax.fori_loop(0, 10, one_block, 0)


def middle_kernel(rank_ref, table_ref, coef_ref, start_ref, q0, q1, q2, q3, mid_ref, edge_ref, u1, u2, h1, h2, pz_ref, py1, py2):
    assemble(rank_ref, table_ref, start_ref, (q0, q1, q2, q3), (u1, u2), (h1, h2))
    z_partners((u1, u2), pz_ref)
    y_partners(u1, py1, h1)
    y_partners(u2, py2, h2)
    states = {1: u1, 2: u2}

    def one_tile(t, carry):
        rates_tile(t, states, (1, 2), (1, 2), pz_ref, (py1, py2), mid_ref, coef_ref, extra=((0, 3), edge_ref))
        return carry

    lax.fori_loop(0, TILES, one_tile, 0)


def join_kernel(rank_ref, table_ref, start_ref, q0, q1, q2, q3, mid_ref, u0, u3, h0, h3, o0, o1, o2, o3, r_ref):
    assemble(rank_ref, table_ref, start_ref, (q0, q1, q2, q3), (u0, u3), (h0, h3))

    def one_tile(t, carry):
        def start(v, a, r):
            return mid_ref[t, v * 2 + a - 1, 8 * r : 8 * r + 8, :]

        def emit(v, a, r, value):
            r_ref[t, v * 2 + a - 1, 8 * r : 8 * r + 8, :] = value

        volume_tile(t, {0: u0, 3: u3}, {1: False, 2: False}, None, start, emit)
        return carry

    lax.fori_loop(0, TILES, one_tile, 0)
    send_increments(rank_ref, table_ref, r_ref, (o0, o1, o2, o3))


def last_kernel(rank_ref, table_ref, coef_ref, u0, u3, h0, h3, partial_ref, left_ref, right_ref, o0, o1, o2, o3, r_ref, pz_ref, py0, py3):
    z_partners((u0, u3), pz_ref)
    y_partners(u0, py0, h0)
    y_partners(u3, py3, h3)
    states = {0: u0, 3: u3}

    def one_tile(t, carry):
        rates_tile(t, states, (0, 3), (0, 3), pz_ref, (py0, py3), r_ref, coef_ref, added=partial_ref)
        x_face_tile(u0, left_ref, r_ref, 0, t)
        x_face_tile(u3, right_ref, r_ref, 1, t)
        return carry

    lax.fori_loop(0, TILES, one_tile, 0)
    send_increments(rank_ref, table_ref, r_ref, (o0, o1, o2, o3))


def finish(rank_ref, pieces, out_hbm, order_ref, stage_ref, sems, pair):
    rank = rank_ref[0]
    for d in range(4):
        slot = lax.rem(rank + 4 - d, 4)
        order_ref[slot] = pieces[d][...]
    copies = []
    for v in range(5):
        for which in range(2):
            n = v * 2 + which
            for half in range(2):
                blocks = [[order_ref[2 * half + k, 5 * n + i] for i in range(5)] for k in range(2)]
                tiles = unpack_pair(*blocks)
                for i in range(5):
                    for r in range(2):
                        stage_ref[pl.ds(n * 160 + 80 * r + 5 * half + i, 8, stride=10), :] = tiles[i][r]
            copy = pltpu.make_async_copy(
                stage_ref.at[pl.ds(n * 160, 160)],
                out_hbm.at[pl.ds((v * 4 + pair[which]) * 160, 160)],
                sems.at[n],
            )
            copy.start()
            copies.append(copy)
    for copy in copies:
        copy.wait()


def finish_middle(rank_ref, q0, q1, q2, q3, out_hbm, order_ref, stage_ref, sems):
    finish(rank_ref, (q0, q1, q2, q3), out_hbm, order_ref, stage_ref, sems, (1, 2))


def finish_edge(rank_ref, q0, q1, q2, q3, before_hbm, out_hbm, order_ref, stage_ref, sems):
    finish(rank_ref, (q0, q1, q2, q3), out_hbm, order_ref, stage_ref, sems, (0, 3))


def f32(*shape):
    return jax.ShapeDtypeStruct(shape, jnp.float32)


TRACE = (TILES, 5, 16, 128)
SIDE = (TILES, 5, 8, 128)
RATE = (TILES, 10, 16, 128)
HALO = (4, 5, 8, 128)
FLAT = (3200, 128)
MESSAGE = (HALO_ROWS, 8, 128)
PIECE = (PACK_ROWS, 8, 128)


def call(kernel, outs, args, scratch=(), flops=0, aliases=None):
    place = {
        "s": pl.BlockSpec(memory_space=pltpu.SMEM),
        "v": pl.BlockSpec(memory_space=pltpu.VMEM),
        "h": pl.BlockSpec(memory_space=pl.ANY),
    }
    moved = sum(4 * math.prod(a.shape) for _, a in args)
    moved += sum(4 * math.prod(shape) for _, shape in outs)
    result = pl.pallas_call(
        kernel,
        out_shape=[f32(*shape) for _, shape in outs],
        in_specs=[place[where] for where, _ in args],
        out_specs=[place[where] for where, _ in outs],
        scratch_shapes=[
            pltpu.SemaphoreType.DMA(shape) if len(shape) == 1 else pltpu.VMEM(shape, jnp.float32)
            for shape in scratch
        ],
        input_output_aliases=aliases or {},
        compiler_params=pltpu.CompilerParams(vmem_limit_bytes=VMEM_LIMIT),
        cost_estimate=pl.CostEstimate(flops=flops, bytes_accessed=moved, transcendentals=0),
    )(*[a for _, a in args])
    return result


def shifted(block, axis, distance):
    count = lax.axis_size(axis)
    return lax.ppermute(block, axis, [((i - distance) % count, i) for i in range(count)])


def v(*arrays):
    return [("v", a) for a in arrays]


def exchange(messages):
    return [shifted(messages[d - 1], "node", d) for d in (1, 2, 3)]


def body(start_state, node_offset):
    start_flat = start_state.reshape(FLAT)
    offset_flat = node_offset.reshape(FLAT)
    rank = ("s", lax.axis_index("node").astype(jnp.int32).reshape(1))
    table = ("s", jnp.asarray(QUAD.reshape(16)))
    coef = ("v", jnp.asarray(coefficient_table()))

    u0, u1, u2, u3, mid, *sent = call(
        front_kernel,
        v(TRACE, TRACE, TRACE, TRACE, RATE, MESSAGE, MESSAGE, MESSAGE),
        [rank, coef, ("h", start_flat), ("h", offset_flat)],
        scratch=[FLAT, FLAT, TRACE, SIDE, SIDE, (10,)],
    )
    got_mid = exchange(sent)
    left = shifted(u3, "space", 1)
    right = shifted(u0, "space", -1)
    *sent, edge = call(
        edge_kernel,
        v(MESSAGE, MESSAGE, MESSAGE, RATE),
        [rank, coef] + v(u0, u1, u2, u3, left, right),
        scratch=[TRACE, SIDE, SIDE],
    )
    got_edge = exchange(sent)
    start_mid, start_edge, own_mid, own_edge = call(
        own_kernel,
        v(MESSAGE, MESSAGE, MESSAGE, MESSAGE),
        [rank] + v(start_flat, mid, edge),
    )
    mid, edge = call(
        middle_kernel,
        v(RATE, RATE),
        [rank, table, coef] + v(start_mid, own_mid, *got_mid),
        scratch=[TRACE, TRACE, HALO, HALO, TRACE, SIDE, SIDE],
    )
    u0, u3, h0, h3, own_mid, *sent = call(
        join_kernel,
        v(TRACE, TRACE, HALO, HALO, PIECE, PIECE, PIECE, PIECE),
        [rank, table] + v(start_edge, own_edge, *got_edge, mid),
        scratch=[RATE],
    )
    got_mid = exchange(sent)
    left = shifted(u3, "space", 1)
    right = shifted(u0, "space", -1)
    own_edge, *sent = call(
        last_kernel,
        v(PIECE, PIECE, PIECE, PIECE),
        [rank, table, coef] + v(u0, u3, h0, h3, edge, left, right),
        scratch=[RATE, TRACE, SIDE, SIDE],
    )
    got_edge = exchange(sent)
    finishing = [(4,) + PIECE, (1600, 128), (10,)]
    (result,) = call(
        finish_middle,
        [("h", FLAT)],
        [rank] + v(own_mid, *got_mid),
        scratch=finishing,
    )
    (result,) = call(
        finish_edge,
        [("h", FLAT)],
        [rank] + v(own_edge, *got_edge) + [("h", result)],
        scratch=finishing,
        aliases={5: 0},
    )
    return result.reshape(node_offset.shape)


def solution(mesh):
    return jax.shard_map(
        body,
        mesh=mesh,
        in_specs=(
            P(None, None, None, None, "space", None),
            P("node", None, None, None, None, "space", None),
        ),
        out_specs=P("node", None, None, None, None, "space", None),
        check_vma=False,
    )
```

```python
import functools
import math

import jax
import jax.numpy as jnp
import numpy as np
from jax import lax
from jax.experimental import pallas as pl
from jax.experimental.pallas import tpu as pltpu
from jax.sharding import PartitionSpec as P

EZ = 80
QUARTER = 320
TILES = 10
ITERS = 2
gamma_gas = 1.4
step_length = 0.01
VMEM_LIMIT = 48 * 1024 * 1024


def lobatto_derivative():
    points = np.array([-1.0, -math.sqrt(0.2), math.sqrt(0.2), 1.0])
    barycentric = np.ones(4)
    for i in range(4):
        for k in range(4):
            if k != i:
                barycentric[i] = barycentric[i] / (points[i] - points[k])
    derivative = np.zeros((4, 4))
    for i in range(4):
        for j in range(4):
            if i != j:
                derivative[i, j] = barycentric[j] / barycentric[i] / (points[i] - points[j])
        derivative[i, i] = -np.sum(derivative[i])
    return derivative


def collocation_matrix():
    near_root = math.sqrt(3.0 / 7 - 2.0 / 7 * math.sqrt(1.2))
    far_root = math.sqrt(3.0 / 7 + 2.0 / 7 * math.sqrt(1.2))
    time_nodes = [(1.0 + value) / 2 for value in (-far_root, -near_root, near_root, far_root)]
    quad_table = np.zeros((4, 4))
    for j in range(4):
        coeffs = [1.0]
        for k in range(4):
            if k != j:
                scale = 1.0 / (time_nodes[j] - time_nodes[k])
                widened = [0.0] * (len(coeffs) + 1)
                for power in range(len(coeffs)):
                    widened[power + 1] = widened[power + 1] + coeffs[power] * scale
                    widened[power] = widened[power] - time_nodes[k] * coeffs[power] * scale
                coeffs = widened
        for m in range(4):
            total = 0.0
            for power in range(len(coeffs)):
                total = total + coeffs[power] * time_nodes[m] ** (power + 1) / (power + 1)
            quad_table[m, j] = total
    return quad_table


DERIV = np.float32(lobatto_derivative())
QUAD = np.float32(step_length * collocation_matrix())
VREG = (8, 128)


def lanes():
    return lax.broadcasted_iota(jnp.int32, VREG, 1)


def sublanes():
    return lax.broadcasted_iota(jnp.int32, VREG, 0)


def lane_roll(tiles, shift):
    count = len(tiles)
    whole, rest = divmod(shift % (128 * count), 128)
    if rest == 0:
        return [tiles[(t - whole) % count] for t in range(count)]
    rotated = [pltpu.roll(tile, rest, 1) for tile in tiles]
    lane = lanes()
    return [
        jnp.where(lane < rest, rotated[(t - whole - 1) % count], rotated[(t - whole) % count])
        for t in range(count)
    ]


def primitive(state):
    rho, m1, m2, m3, energy = state
    inverse = 1.0 / rho
    v1, v2, v3 = m1 * inverse, m2 * inverse, m3 * inverse
    pressure = (gamma_gas - 1.0) * (energy - 0.5 * (m1 * v1 + m2 * v2 + m3 * v3))
    return inverse, (v1, v2, v3), pressure


def flux_entry(state, velocity, pressure, variable, direction):
    speed = velocity[direction]
    if variable == 0:
        return state[1 + direction]
    if variable == 4:
        return (state[4] + pressure) * speed
    entry = state[variable] * speed
    if variable - 1 == direction:
        entry = entry + pressure
    return entry


def wave(inverse, velocity, pressure, direction):
    square = gamma_gas * pressure * inverse
    return jnp.abs(velocity[direction]) + square * lax.rsqrt(square)


def face_terms(own, other, direction, sign):
    own_inv, own_v, own_p = primitive(own)
    oth_inv, oth_v, oth_p = primitive(other)
    speed = 3.0 * jnp.maximum(
        wave(own_inv, own_v, own_p, direction), wave(oth_inv, oth_v, oth_p, direction)
    )
    weight = 3.0 * sign
    terms = []
    for variable in range(5):
        jump = other[variable] - own[variable]
        flux_jump = flux_entry(own, own_v, own_p, variable, direction) - flux_entry(
            other, oth_v, oth_p, variable, direction
        )
        terms.append(speed * jump + weight * flux_jump)
    return terms


def z_partners(pair, pz_ref):
    lane = lanes()
    slot = sublanes() % 4
    even_ref, odd_ref = pair

    def one_variable(v, carry):
        for r in range(2):
            rows = slice(8 * r, 8 * r + 8)
            mixed = []
            for t in range(TILES):
                even = even_ref[t, v, rows, :]
                odd = odd_ref[t, v, rows, :]
                low = jnp.where(slot == 0, pltpu.roll(even, 5, 0), pltpu.roll(odd, 6, 0))
                high = jnp.where(slot == 3, pltpu.roll(even, 3, 0), pltpu.roll(odd, 2, 0))
                mixed.append(jnp.where(slot < 2, low, high))
            before = lane_roll(mixed, 1)
            before_wrap = lane_roll(mixed, -(EZ - 1))
            after = lane_roll(mixed, -1)
            after_wrap = lane_roll(mixed, EZ - 1)
            for t in range(TILES):
                column = (lane + 128 * t) % EZ
                low = jnp.where(column == 0, before_wrap[t], before[t])
                high = jnp.where(column == EZ - 1, after_wrap[t], after[t])
                pz_ref[t, v, rows, :] = jnp.where(slot < 2, low, high)
        return carry

    lax.fori_loop(0, 5, one_variable, 0)


def y_partners(u_ref, py_ref, halo_ref=None):
    lane = lanes()
    lower = sublanes() < 4

    def one_variable(v, carry):
        swapped = []
        for t in range(TILES):
            trace = jnp.where(lower, u_ref[t, v, 0:8, :], u_ref[t, v, 8:16, :])
            swapped.append(pltpu.roll(trace, 4, 0))
        before = lane_roll(swapped, EZ)
        after = lane_roll(swapped, -EZ)
        if halo_ref is not None:
            for m in range(4):
                base = 5 * (m // 2)
                got = pltpu.roll(halo_ref[m, v], 4, 0)
                if m % 2 == 0:
                    before[base] = jnp.where(lane < 80, got, before[base])
                    moved = pltpu.roll(got, 112, 1)
                    after[base + 1] = jnp.where(lane >= 112, moved, after[base + 1])
                    after[base + 2] = jnp.where(lane < 64, moved, after[base + 2])
                else:
                    moved = pltpu.roll(got, 64, 1)
                    before[base + 2] = jnp.where(lane >= 64, moved, before[base + 2])
                    before[base + 3] = jnp.where(lane < 16, moved, before[base + 3])
                    moved = pltpu.roll(got, 48, 1)
                    after[base + 4] = jnp.where(lane >= 48, moved, after[base + 4])
        for t in range(TILES):
            py_ref[t, v] = jnp.where(lower, before[t], after[t])
        return carry

    lax.fori_loop(0, 5, one_variable, 0)


def load_state(u_ref, t, rows):
    return [u_ref[t, v, rows, :] for v in range(5)]


def z_face_terms(pair, pz_ref, t):
    slot = sublanes() % 4
    outer = (slot == 0) | (slot == 3)
    sign = jnp.where(slot < 2, -1.0, 1.0).astype(jnp.float32)
    result = [[[None, None] for _ in range(2)] for _ in range(5)]
    for r in range(2):
        rows = slice(8 * r, 8 * r + 8)
        own, other = [], []
        for v in range(5):
            even = pair[0][t, v, rows, :]
            odd = pair[1][t, v, rows, :]
            inner = jnp.where(slot == 1, pltpu.roll(odd, 1, 0), pltpu.roll(odd, 7, 0))
            own.append(jnp.where(outer, even, inner))
            other.append(pz_ref[t, v, rows, :])
        terms = face_terms(own, other, 2, sign)
        for v in range(5):
            term = terms[v]
            result[v][0][r] = jnp.where(outer, term, 0.0)
            moved = jnp.where(slot == 0, pltpu.roll(term, 7, 0), pltpu.roll(term, 1, 0))
            result[v][1][r] = jnp.where(outer, moved, 0.0)
    return result


def volume_tile(t, states, targets, coef_ref, start, emit, halves=(0, 1)):
    slot = sublanes() % 4
    state, prim = {}, {}
    for a, ref in states.items():
        for r in halves:
            rows = slice(8 * r, 8 * r + 8) if ref.shape[2] == 16 else slice(0, 8)
            state[a, r] = load_state(ref, t, rows)
            prim[a, r] = primitive(state[a, r])

    def flux(a, r, v, direction):
        return flux_entry(state[a, r], prim[a, r][1], prim[a, r][2], v, direction)

    for v in range(5):
        total = {}
        for r in halves:
            column = {a: flux(a, r, v, 0) for a in states}
            for a in targets:
                value = start(v, a, r)
                for other in states:
                    term = float(-DERIV[a, other]) * column[other]
                    value = term if value is None else value + term
                total[a, r] = value
        for a, whole in targets.items():
            if whole:
                first, second = flux(a, 0, v, 1), flux(a, 1, v, 1)
                parts = [first, pltpu.roll(first, 4, 0), second, pltpu.roll(second, 4, 0)]
                for r in range(2):
                    for k in range(4):
                        total[a, r] = total[a, r] - coef_ref[4 * r + k] * parts[k]
            for r in halves:
                acc = total[a, r]
                if whole:
                    along = flux(a, r, v, 2)
                    across = pltpu.roll(along, 4, 0)
                    acc = acc - coef_ref[8] * along
                    for shift in range(1, 4):
                        mixed = pltpu.roll(jnp.where(slot < 4 - shift, along, across), shift, 0)
                        acc = acc - coef_ref[8 + shift] * mixed
                emit(v, a, r, acc)


def sublane_column(values):
    row = sublanes()
    block = jnp.full(VREG, float(values[0]), jnp.float32)
    for s in range(1, 8):
        if values[s] != values[s - 1]:
            block = jnp.where(row >= s, float(values[s]), block)
    return block


def fill_coefficients(coef_ref):
    table = np.zeros((12, 8), np.float32)
    for row in range(8):
        group, c = divmod(row, 4)
        for r in range(2):
            for k in range(4):
                source = 2 * (k // 2) + (group if k % 2 == 0 else 1 - group)
                table[4 * r + k, row] = DERIV[2 * r + group, source]
        for shift in range(4):
            table[8 + shift, row] = DERIV[c, (c - shift) % 4]
    for i in range(12):
        coef_ref[i] = sublane_column(table[i])


def y_face_tile(u_ref, py_ref, r_ref, which, t):
    lower = sublanes() < 4
    sign = jnp.where(lower, -1.0, 1.0).astype(jnp.float32)
    own = [jnp.where(lower, u_ref[t, v, 0:8, :], u_ref[t, v, 8:16, :]) for v in range(5)]
    terms = face_terms(own, [py_ref[t, v] for v in range(5)], 1, sign)
    for v in range(5):
        r_ref[t, v * 2 + which, 0:8, :] += jnp.where(lower, terms[v], 0.0)
        r_ref[t, v * 2 + which, 8:16, :] += jnp.where(lower, 0.0, terms[v])


def x_face_tile(u_ref, other_ref, r_ref, which, t):
    sign = -1.0 if which == 0 else 1.0
    for r in range(2):
        rows = slice(8 * r, 8 * r + 8)
        terms = face_terms(load_state(u_ref, t, rows), load_state(other_ref, t, rows), 0, sign)
        for v in range(5):
            r_ref[t, v * 2 + which, rows, :] += terms[v]


def rates_tile(t, states, pair, sources, pz_ref, py_refs, r_ref, coef_ref, added=None, extra=None):
    targets = {a: True for a in pair}
    refs = [states[a] for a in pair]
    face = z_face_terms(refs, pz_ref, t)

    def start(v, a, r):
        if a not in pair:
            return None
        which = pair.index(a)
        value = face[v][which][r]
        if added is not None:
            value = value + added[t, v * 2 + which, 8 * r : 8 * r + 8, :]
        return value

    def emit(v, a, r, value):
        if a in pair:
            r_ref[t, v * 2 + pair.index(a), 8 * r : 8 * r + 8, :] = value
        else:
            extra[1][t, v * 2 + extra[0].index(a), 8 * r : 8 * r + 8, :] = value

    if extra is not None:
        targets.update({a: False for a in extra[0]})
    volume_tile(t, {a: states[a] for a in sources}, targets, coef_ref, start, emit)
    for which in range(2):
        y_face_tile(refs[which], py_refs[which], r_ref, which, t)


def pack_pair(tiles):
    lane = lanes()
    low = lane < 64
    flip = [[pltpu.roll(half, 64, 1) for half in tile] for tile in tiles]
    first = [
        tiles[0][0],
        tiles[1][0],
        tiles[0][1],
        tiles[1][1],
        jnp.where(low, tiles[2][0], flip[2][1]),
    ]
    second = [
        jnp.where(low, flip[2][0], flip[3][0]),
        jnp.where(low, flip[3][0], flip[4][0]),
        jnp.where(low, flip[2][1], flip[3][1]),
        jnp.where(low, flip[3][1], flip[4][1]),
        jnp.where(low, flip[4][0], tiles[4][1]),
    ]
    return first, second


def unpack_pair(first, second):
    low = lanes() < 64
    flip_first = pltpu.roll(first[4], 64, 1)
    flip = [pltpu.roll(block, 64, 1) for block in second]
    return [
        [first[0], first[2]],
        [first[1], first[3]],
        [jnp.where(low, first[4], flip[0]), jnp.where(low, flip_first, flip[2])],
        [jnp.where(low, flip[0], flip[1]), jnp.where(low, flip[2], flip[3])],
        [jnp.where(low, flip[1], flip[4]), jnp.where(low, flip[3], second[4])],
    ]


HALF_ROWS = 25
PACK_ROWS = 50
HALO_ROWS = 57


def pack_halo_parts(halos):
    lane = lanes()
    packed = [
        jnp.where(lane < 64, halos[2 * v], pltpu.roll(halos[2 * v + 1], 64, 1)) for v in range(5)
    ]
    for first in (0, 8):
        block = None
        for n in range(first, min(first + 8, 10)):
            moved = pltpu.roll(halos[n], (16 * (n - first) + 64) % 128, 1)
            block = moved if block is None else jnp.where(lane < 16 * (n - first), block, moved)
        packed.append(block)
    return packed


def unpack_halo_parts(packed):
    lane = lanes()
    halos = []
    for n in range(10):
        low = packed[n // 2] if n % 2 == 0 else pltpu.roll(packed[n // 2], 64, 1)
        rest = pltpu.roll(packed[5 + n // 8], (64 - 16 * (n % 8)) % 128, 1)
        halos.append(jnp.where(lane < 64, low, rest))
    return halos


def pack_message(load, quarter, put):
    lane = lanes()
    low = lane < 64
    lower = sublanes() < 4
    odd = quarter % 2
    base = (5 * quarter) // 2
    shift = 64 * odd
    keep = lane < 128 - shift
    under = lax.rem(base + 9, 10)
    over = lax.rem(base + 3, 10)
    below_shift = 80 - 64 * odd
    above_shift = 64 - 64 * odd
    halos = [None] * 10
    for v in range(5):
        tops = []
        for r in range(2):
            blocks = [[load(which, v, r, base + i) for i in range(3)] for which in range(2)]
            turned = [[pltpu.roll(x, shift, 1) for x in half] for half in blocks]
            first = (5 * r + v) * 5
            for which in range(2):
                put(first + 2 * which, jnp.where(keep, turned[which][0], turned[which][1]))
                put(first + 2 * which + 1, jnp.where(keep, turned[which][1], turned[which][2]))
            put(first + 4, jnp.where(low, turned[0][2], pltpu.roll(blocks[1][2], above_shift, 1)))
            tops.append(blocks)
        for which in range(2):
            below = jnp.where(
                lane < below_shift,
                pltpu.roll(load(which, v, 1, under), below_shift, 1),
                pltpu.roll(tops[1][which][0], below_shift, 1),
            )
            above = jnp.where(
                lane < above_shift,
                pltpu.roll(tops[0][which][2], above_shift, 1),
                pltpu.roll(load(which, v, 0, over), above_shift, 1),
            )
            halos[2 * v + which] = jnp.where(lower, above, below)
    for i, block in enumerate(pack_halo_parts(halos)):
        put(PACK_ROWS + i, block)


def rate_loader(r_ref):
    return lambda which, v, r, t: r_ref[t, v * 2 + which, 8 * r : 8 * r + 8, :]


def writer(*refs):
    def put(row, block):
        for ref in refs:
            if row < ref.shape[0]:
                ref[row] = block
                return
            row -= ref.shape[0]

    return put


def start_rows(v, a, r, t):
    return pl.ds(((v * 4 + a) * 16 + 8 * r) * 10 + t, 8, stride=10)


def front_kernel(rank_ref, start_hbm, offset_hbm, u0, u1, u2, u3, r_ref, m1, m2, m3, start_ref, offset_ref, pz_ref, py1, py2, coef_ref, sems):
    copies = []
    for v in range(5):
        rows = pl.ds(640 * v, 640)
        pair = [
            pltpu.make_async_copy(start_hbm.at[rows], start_ref.at[rows], sems.at[2 * v]),
            pltpu.make_async_copy(offset_hbm.at[rows], offset_ref.at[rows], sems.at[2 * v + 1]),
        ]
        for copy in pair:
            copy.start()
        copies.append(pair)
    states = {0: u0, 1: u1, 2: u2, 3: u3}
    fill_coefficients(coef_ref)
    for v in range(5):
        for copy in copies[v]:
            copy.wait()
        rows = slice(640 * v, 640 * v + 640)
        offset_ref[rows, :] = offset_ref[rows, :] + start_ref[rows, :]
        for a in range(4):
            for t in range(TILES):
                for r in range(2):
                    states[a][t, v, 8 * r : 8 * r + 8, :] = offset_ref[start_rows(v, a, r, t), :]
    z_partners((u1, u2), pz_ref)
    y_partners(u1, py1)
    y_partners(u2, py2)

    def one_tile(t, carry):
        rates_tile(t, states, (1, 2), (0, 1, 2, 3), pz_ref, (py1, py2), r_ref, coef_ref)
        return carry

    lax.fori_loop(0, TILES, one_tile, 0)
    for d, out in ((1, m1), (2, m2), (3, m3)):
        pack_message(rate_loader(r_ref), lax.rem(rank_ref[0] + d, 4), writer(out))


def edge_kernel(rank_ref, u0, u1, u2, u3, left_ref, right_ref, t1, t2, t3, m1, m2, m3, r_ref, pz_ref, py0, py3, coef_ref):
    fill_coefficients(coef_ref)
    z_partners((u0, u3), pz_ref)
    y_partners(u0, py0)
    y_partners(u3, py3)
    states = {0: u0, 1: u1, 2: u2, 3: u3}

    def one_tile(t, carry):
        rates_tile(t, states, (0, 3), (0, 1, 2, 3), pz_ref, (py0, py3), r_ref, coef_ref)
        x_face_tile(u0, left_ref, r_ref, 0, t)
        x_face_tile(u3, right_ref, r_ref, 1, t)
        return carry

    lax.fori_loop(0, TILES, one_tile, 0)
    for d, outs in ((1, (t1, m1)), (2, (t2, m2)), (3, (t3, m3))):
        pack_message(rate_loader(r_ref), lax.rem(rank_ref[0] + d, 4), writer(*outs))


def own_kernel(rank_ref, start_ref, mid_ref, edge_ref, start_mid, start_edge, own_mid, own_edge):
    rank = rank_ref[0]
    for pair, rates, start_out, own_out in (((1, 2), mid_ref, start_mid, own_mid), ((0, 3), edge_ref, start_edge, own_edge)):

        def load(which, v, r, t):
            return start_ref[start_rows(v, pair[which], r, t), :]

        pack_message(load, rank, writer(start_out))
        pack_message(rate_loader(rates), rank, writer(own_out))


def assemble(rank_ref, table_ref, start_ref, rates, skipped, halves, states, halos=None):
    rank = rank_ref[0]
    weight = [
        [table_ref[m * 4 + lax.rem(rank + 4 - d, 4)] for d in range(4)] for m in range(4)
    ]

    def node_state(m, row):
        total = start_ref[row] + weight[m][0] * rates[0][row]
        for d in range(1, 4):
            total = total + weight[m][d] * rates[d][row - skipped]
        return total

    def one_variable(v, carry):
        for r in halves:
            first = (5 * r + v) * 5
            for pair in range(2):
                pieces = [[node_state(2 * pair + half, first + i) for i in range(5)] for half in range(2)]
                tiles = unpack_pair(*pieces)
                for i in range(5):
                    for which in range(2):
                        ref = states[which]
                        rows = slice(8 * r, 8 * r + 8) if ref.shape[2] == 16 else slice(0, 8)
                        ref[5 * pair + i, v, rows, :] = tiles[i][which]
        return carry

    lax.fori_loop(0, 5, one_variable, 0)
    if halos is not None:
        for m in range(4):
            blocks = unpack_halo_parts([node_state(m, PACK_ROWS + i) for i in range(7)])
            for n in range(10):
                halos[n % 2][m, n // 2] = blocks[n]


def send_increments(rank_ref, table_ref, r_ref, halves, outs):
    rank = rank_ref[0]
    weight = [[table_ref[lax.rem(rank + d, 4) * 4 + j] for j in range(4)] for d in range(4)]

    def one_variable(v, carry):
        for place, r in enumerate(halves):
            rows = slice(8 * r, 8 * r + 8) if r_ref.shape[2] == 16 else slice(0, 8)
            pieces = []
            for pair in range(2):
                tiles = [[r_ref[5 * pair + i, 2 * v + which, rows, :] for which in range(2)] for i in range(5)]
                pieces.extend(pack_pair(tiles))
            for d in range(4):
                for i in range(5):
                    total = weight[d][0] * pieces[0][i]
                    for j in range(1, 4):
                        total = total + weight[d][j] * pieces[j][i]
                    outs[d][(5 * place + v) * 5 + i] = total
        return carry

    lax.fori_loop(0, 5, one_variable, 0)


def middle_kernel(rank_ref, table_ref, start_ref, q0, q1, q2, q3, mid_ref, edge_ref, u1, u2, h1, h2, pz_ref, py1, py2, coef_ref):
    fill_coefficients(coef_ref)
    assemble(rank_ref, table_ref, start_ref, (q0, q1, q2, q3), 0, (0, 1), (u1, u2), (h1, h2))
    z_partners((u1, u2), pz_ref)
    y_partners(u1, py1, h1)
    y_partners(u2, py2, h2)
    states = {1: u1, 2: u2}

    def one_tile(t, carry):
        rates_tile(t, states, (1, 2), (1, 2), pz_ref, (py1, py2), mid_ref, coef_ref, extra=((0, 3), edge_ref))
        return carry

    lax.fori_loop(0, TILES, one_tile, 0)


def complete_middle(rank_ref, table_ref, mid_ref, u0, u3, r, r_ref, outs):
    def one_tile(t, carry):
        def start(v, a, half):
            return mid_ref[t, v * 2 + a - 1, 8 * half : 8 * half + 8, :]

        def emit(v, a, half, value):
            r_ref[t, v * 2 + a - 1] = value

        volume_tile(t, {0: u0, 3: u3}, {1: False, 2: False}, None, start, emit, (r,))
        return carry

    lax.fori_loop(0, TILES, one_tile, 0)
    send_increments(rank_ref, table_ref, r_ref, (r,), outs)


def upper_kernel(rank_ref, table_ref, start_ref, q0, q1, q2, q3, mid_ref, w0, w3, o0, o1, o2, o3, r_ref):
    assemble(rank_ref, table_ref, start_ref, (q0, q1, q2, q3), 0, (0,), (w0, w3))
    complete_middle(rank_ref, table_ref, mid_ref, w0, w3, 0, r_ref, (o0, o1, o2, o3))


def lower_kernel(rank_ref, table_ref, start_ref, q0, q1, q2, q3, mid_ref, w0, w3, u0, u3, h0, h3, o0, o1, o2, o3, r_ref):
    assemble(rank_ref, table_ref, start_ref, (q0, q1, q2, q3), HALF_ROWS, (1,), (u0, u3), (h0, h3))
    u0[:, :, 0:8, :] = w0[...]
    u3[:, :, 0:8, :] = w3[...]
    complete_middle(rank_ref, table_ref, mid_ref, u0, u3, 1, r_ref, (o0, o1, o2, o3))


def last_inner_kernel(u0, u3, h0, h3, partial_ref, r_ref, pz_ref, py0, py3, coef_ref):
    fill_coefficients(coef_ref)
    z_partners((u0, u3), pz_ref)
    y_partners(u0, py0, h0)
    y_partners(u3, py3, h3)
    states = {0: u0, 3: u3}

    def one_tile(t, carry):
        rates_tile(t, states, (0, 3), (0, 3), pz_ref, (py0, py3), r_ref, coef_ref, added=partial_ref)
        return carry

    lax.fori_loop(0, TILES, one_tile, 0)


def last_outer_kernel(rank_ref, table_ref, u0, u3, inner_ref, left_ref, right_ref, o0, o1, o2, o3, r_ref):
    def one_tile(t, carry):
        r_ref[t] = inner_ref[t]
        x_face_tile(u0, left_ref, r_ref, 0, t)
        x_face_tile(u3, right_ref, r_ref, 1, t)
        return carry

    lax.fori_loop(0, TILES, one_tile, 0)
    send_increments(rank_ref, table_ref, r_ref, (0, 1), (o0, o1, o2, o3))


def finish(rank_ref, halves, out_hbm, order_ref, stage_ref, sems, pair):
    rank = rank_ref[0]
    count = PACK_ROWS // len(halves)
    for place, pieces in enumerate(halves):
        for d in range(4):
            slot = lax.rem(rank + 4 - d, 4)
            order_ref[slot, count * place : count * (place + 1)] = pieces[d][...]
    copies = []
    for v in range(5):
        for r in range(2):
            for half in range(2):
                first = (5 * r + v) * 5
                blocks = [[order_ref[2 * half + k, first + i] for i in range(5)] for k in range(2)]
                tiles = unpack_pair(*blocks)
                for i in range(5):
                    for which in range(2):
                        row = (v * 2 + which) * 160 + 80 * r + 5 * half + i
                        stage_ref[pl.ds(row, 8, stride=10), :] = tiles[i][which]
        for which in range(2):
            n = v * 2 + which
            copy = pltpu.make_async_copy(
                stage_ref.at[pl.ds(n * 160, 160)],
                out_hbm.at[pl.ds((v * 4 + pair[which]) * 160, 160)],
                sems.at[n],
            )
            copy.start()
            copies.append(copy)
    for copy in copies:
        copy.wait()


def finish_middle(rank_ref, a0, a1, a2, a3, b0, b1, b2, b3, out_hbm, order_ref, stage_ref, sems):
    finish(rank_ref, ((a0, a1, a2, a3), (b0, b1, b2, b3)), out_hbm, order_ref, stage_ref, sems, (1, 2))


def finish_edge(rank_ref, q0, q1, q2, q3, before_hbm, out_hbm, order_ref, stage_ref, sems):
    finish(rank_ref, ((q0, q1, q2, q3),), out_hbm, order_ref, stage_ref, sems, (0, 3))


def f32(*shape):
    return jax.ShapeDtypeStruct(shape, jnp.float32)


TRACE = (TILES, 5, 16, 128)
SIDE = (TILES, 5, 8, 128)
RATE = (TILES, 10, 16, 128)
HALO = (4, 5, 8, 128)
FLAT = (3200, 128)
MESSAGE = (HALO_ROWS, 8, 128)
PIECE = (PACK_ROWS, 8, 128)
UPPER = (HALF_ROWS, 8, 128)
LOWER = (HALO_ROWS - HALF_ROWS, 8, 128)
HALF = (TILES, 10, 8, 128)
COEF = (12, 8, 128)


def call(kernel, outs, args, scratch=(), flops=0, aliases=None):
    place = {
        "s": pl.BlockSpec(memory_space=pltpu.SMEM),
        "v": pl.BlockSpec(memory_space=pltpu.VMEM),
        "h": pl.BlockSpec(memory_space=pltpu.HBM),
    }
    moved = sum(4 * math.prod(a.shape) for _, a in args)
    moved += sum(4 * math.prod(shape) for _, shape in outs)
    result = pl.pallas_call(
        kernel,
        out_shape=[f32(*shape) for _, shape in outs],
        in_specs=[place[where] for where, _ in args],
        out_specs=[place[where] for where, _ in outs],
        scratch_shapes=[
            pltpu.SemaphoreType.DMA(shape) if len(shape) == 1 else pltpu.VMEM(shape, jnp.float32)
            for shape in scratch
        ],
        input_output_aliases=aliases or {},
        compiler_params=pltpu.CompilerParams(vmem_limit_bytes=VMEM_LIMIT),
        cost_estimate=pl.CostEstimate(flops=flops, bytes_accessed=1, transcendentals=0),
    )(*[a for _, a in args])
    return result


def shifted(block, axis, distance):
    count = lax.axis_size(axis)
    return lax.ppermute(block, axis, [((i - distance) % count, i) for i in range(count)])


def v(*arrays):
    return [("v", a) for a in arrays]


def exchange(messages):
    return [shifted(messages[d - 1], "node", d) for d in (1, 2, 3)]


def body(start_state, node_offset):
    start_flat = start_state.reshape(FLAT)
    offset_flat = node_offset.reshape(FLAT)
    rank = ("s", lax.axis_index("node").astype(jnp.int32).reshape(1))
    table = ("s", jnp.asarray(QUAD.reshape(16)))

    u0, u1, u2, u3, mid, *sent = call(
        front_kernel,
        v(TRACE, TRACE, TRACE, TRACE, RATE, MESSAGE, MESSAGE, MESSAGE),
        [rank, ("h", start_flat), ("h", offset_flat)],
        scratch=[FLAT, FLAT, TRACE, SIDE, SIDE, COEF, (10,)],
    )
    got_mid = exchange(sent)
    left = shifted(u3, "space", 1)
    right = shifted(u0, "space", -1)
    *sent, edge = call(
        edge_kernel,
        v(UPPER, UPPER, UPPER, LOWER, LOWER, LOWER, RATE),
        [rank] + v(u0, u1, u2, u3, left, right),
        scratch=[TRACE, SIDE, SIDE, COEF],
    )
    got_upper = exchange(sent[:3])
    got_lower = exchange(sent[3:])
    start_mid, start_edge, own_mid, own_edge = call(
        own_kernel,
        v(MESSAGE, MESSAGE, MESSAGE, MESSAGE),
        [rank] + v(start_flat, mid, edge),
    )
    mid, edge = call(
        middle_kernel,
        v(RATE, RATE),
        [rank, table] + v(start_mid, own_mid, *got_mid),
        scratch=[TRACE, TRACE, HALO, HALO, TRACE, SIDE, SIDE, COEF],
    )
    w0, w3, own_upper, *sent = call(
        upper_kernel,
        v(SIDE, SIDE, UPPER, UPPER, UPPER, UPPER),
        [rank, table] + v(start_edge, own_edge, *got_upper, mid),
        scratch=[HALF],
    )
    got_upper = exchange(sent)
    u0, u3, h0, h3, own_lower, *sent = call(
        lower_kernel,
        v(TRACE, TRACE, HALO, HALO, UPPER, UPPER, UPPER, UPPER),
        [rank, table] + v(start_edge, own_edge, *got_lower, mid, w0, w3),
        scratch=[HALF],
    )
    got_lower = exchange(sent)
    left = shifted(u3, "space", 1)
    right = shifted(u0, "space", -1)
    (inner,) = call(
        last_inner_kernel,
        v(RATE),
        v(u0, u3, h0, h3, edge),
        scratch=[TRACE, SIDE, SIDE, COEF],
    )
    own_edge, *sent = call(
        last_outer_kernel,
        v(PIECE, PIECE, PIECE, PIECE),
        [rank, table] + v(u0, u3, inner, left, right),
        scratch=[RATE],
    )
    got_edge = exchange(sent)
    finishing = [(4,) + PIECE, (1600, 128), (10,)]
    (result,) = call(
        finish_middle,
        [("h", FLAT)],
        [rank] + v(own_upper, *got_upper, own_lower, *got_lower),
        scratch=finishing,
    )
    (result,) = call(
        finish_edge,
        [("h", FLAT)],
        [rank] + v(own_edge, *got_edge) + [("h", result)],
        scratch=finishing,
        aliases={5: 0},
    )
    return result.reshape(node_offset.shape)


def solution(mesh):
    return jax.shard_map(
        body,
        mesh=mesh,
        in_specs=(
            P(None, None, None, None, "space", None),
            P("node", None, None, None, None, "space", None),
        ),
        out_specs=P("node", None, None, None, None, "space", None),
        check_vma=False,
    )
```

```python
import functools
import math

import jax
import jax.numpy as jnp
import numpy as np
from jax import lax
from jax.experimental import pallas as pl
from jax.experimental.pallas import tpu as pltpu
from jax.sharding import PartitionSpec as P

EZ = 80
QUARTER = 320
TILES = 10
ITERS = 2
gamma_gas = 1.4
step_length = 0.01
VMEM_LIMIT = 48 * 1024 * 1024


def lobatto_derivative():
    points = np.array([-1.0, -math.sqrt(0.2), math.sqrt(0.2), 1.0])
    barycentric = np.ones(4)
    for i in range(4):
        for k in range(4):
            if k != i:
                barycentric[i] = barycentric[i] / (points[i] - points[k])
    derivative = np.zeros((4, 4))
    for i in range(4):
        for j in range(4):
            if i != j:
                derivative[i, j] = barycentric[j] / barycentric[i] / (points[i] - points[j])
        derivative[i, i] = -np.sum(derivative[i])
    return derivative


def collocation_matrix():
    near_root = math.sqrt(3.0 / 7 - 2.0 / 7 * math.sqrt(1.2))
    far_root = math.sqrt(3.0 / 7 + 2.0 / 7 * math.sqrt(1.2))
    time_nodes = [(1.0 + value) / 2 for value in (-far_root, -near_root, near_root, far_root)]
    quad_table = np.zeros((4, 4))
    for j in range(4):
        coeffs = [1.0]
        for k in range(4):
            if k != j:
                scale = 1.0 / (time_nodes[j] - time_nodes[k])
                widened = [0.0] * (len(coeffs) + 1)
                for power in range(len(coeffs)):
                    widened[power + 1] = widened[power + 1] + coeffs[power] * scale
                    widened[power] = widened[power] - time_nodes[k] * coeffs[power] * scale
                coeffs = widened
        for m in range(4):
            total = 0.0
            for power in range(len(coeffs)):
                total = total + coeffs[power] * time_nodes[m] ** (power + 1) / (power + 1)
            quad_table[m, j] = total
    return quad_table


DERIV = np.float32(lobatto_derivative())
QUAD = np.float32(step_length * collocation_matrix())
VREG = (8, 128)


def lanes():
    return lax.broadcasted_iota(jnp.int32, VREG, 1)


def sublanes():
    return lax.broadcasted_iota(jnp.int32, VREG, 0)


def lane_roll(tiles, shift):
    count = len(tiles)
    whole, rest = divmod(shift % (128 * count), 128)
    if rest == 0:
        return [tiles[(t - whole) % count] for t in range(count)]
    rotated = [pltpu.roll(tile, rest, 1) for tile in tiles]
    lane = lanes()
    return [
        jnp.where(lane < rest, rotated[(t - whole - 1) % count], rotated[(t - whole) % count])
        for t in range(count)
    ]


def primitive(state):
    rho, m1, m2, m3, energy = state
    inverse = 1.0 / rho
    v1, v2, v3 = m1 * inverse, m2 * inverse, m3 * inverse
    pressure = (gamma_gas - 1.0) * (energy - 0.5 * (m1 * v1 + m2 * v2 + m3 * v3))
    return inverse, (v1, v2, v3), pressure


def flux_entry(state, velocity, pressure, variable, direction):
    speed = velocity[direction]
    if variable == 0:
        return state[1 + direction]
    if variable == 4:
        return (state[4] + pressure) * speed
    entry = state[variable] * speed
    if variable - 1 == direction:
        entry = entry + pressure
    return entry


def wave(inverse, velocity, pressure, direction):
    square = gamma_gas * pressure * inverse
    return jnp.abs(velocity[direction]) + square * lax.rsqrt(square)


def face_terms(own, other, direction, sign):
    own_inv, own_v, own_p = primitive(own)
    oth_inv, oth_v, oth_p = primitive(other)
    speed = 3.0 * jnp.maximum(
        wave(own_inv, own_v, own_p, direction), wave(oth_inv, oth_v, oth_p, direction)
    )
    weight = 3.0 * sign
    terms = []
    for variable in range(5):
        jump = other[variable] - own[variable]
        flux_jump = flux_entry(own, own_v, own_p, variable, direction) - flux_entry(
            other, oth_v, oth_p, variable, direction
        )
        terms.append(speed * jump + weight * flux_jump)
    return terms


def z_partners(pair, pz_ref, only=None):
    lane = lanes()
    slot = sublanes() % 4
    even_ref, odd_ref = pair

    def one_variable(v, carry):
        for r in range(2):
            rows = slice(8 * r, 8 * r + 8)
            mixed = []
            for t in range(TILES):
                even = even_ref[t, v, rows, :]
                odd = odd_ref[t, v, rows, :]
                low = jnp.where(slot == 0, pltpu.roll(even, 5, 0), pltpu.roll(odd, 6, 0))
                high = jnp.where(slot == 3, pltpu.roll(even, 3, 0), pltpu.roll(odd, 2, 0))
                mixed.append(jnp.where(slot < 2, low, high))
            before = lane_roll(mixed, 1)
            before_wrap = lane_roll(mixed, -(EZ - 1))
            after = lane_roll(mixed, -1)
            after_wrap = lane_roll(mixed, EZ - 1)
            for t in range(TILES):
                column = (lane + 128 * t) % EZ
                low = jnp.where(column == 0, before_wrap[t], before[t])
                high = jnp.where(column == EZ - 1, after_wrap[t], after[t])
                pz_ref[t, v, rows, :] = jnp.where(slot < 2, low, high)
        return carry

    if only is None:
        lax.fori_loop(0, 5, one_variable, 0)
    else:
        one_variable(only, 0)


def y_partners(u_ref, py_ref, halo_ref=None, only=None):
    lane = lanes()
    lower = sublanes() < 4

    def one_variable(v, carry):
        swapped = []
        for t in range(TILES):
            trace = jnp.where(lower, u_ref[t, v, 0:8, :], u_ref[t, v, 8:16, :])
            swapped.append(pltpu.roll(trace, 4, 0))
        before = lane_roll(swapped, EZ)
        after = lane_roll(swapped, -EZ)
        if halo_ref is not None:
            for m in range(4):
                base = 5 * (m // 2)
                got = pltpu.roll(halo_ref[m, v], 4, 0)
                if m % 2 == 0:
                    before[base] = jnp.where(lane < 80, got, before[base])
                    moved = pltpu.roll(got, 112, 1)
                    after[base + 1] = jnp.where(lane >= 112, moved, after[base + 1])
                    after[base + 2] = jnp.where(lane < 64, moved, after[base + 2])
                else:
                    moved = pltpu.roll(got, 64, 1)
                    before[base + 2] = jnp.where(lane >= 64, moved, before[base + 2])
                    before[base + 3] = jnp.where(lane < 16, moved, before[base + 3])
                    moved = pltpu.roll(got, 48, 1)
                    after[base + 4] = jnp.where(lane >= 48, moved, after[base + 4])
        for t in range(TILES):
            py_ref[t, v] = jnp.where(lower, before[t], after[t])
        return carry

    if only is None:
        lax.fori_loop(0, 5, one_variable, 0)
    else:
        one_variable(only, 0)


def load_state(u_ref, t, rows):
    return [u_ref[t, v, rows, :] for v in range(5)]


def z_face_terms(pair, pz_ref, t):
    slot = sublanes() % 4
    outer = (slot == 0) | (slot == 3)
    sign = jnp.where(slot < 2, -1.0, 1.0).astype(jnp.float32)
    result = [[[None, None] for _ in range(2)] for _ in range(5)]
    for r in range(2):
        rows = slice(8 * r, 8 * r + 8)
        own, other = [], []
        for v in range(5):
            even = pair[0][t, v, rows, :]
            odd = pair[1][t, v, rows, :]
            inner = jnp.where(slot == 1, pltpu.roll(odd, 1, 0), pltpu.roll(odd, 7, 0))
            own.append(jnp.where(outer, even, inner))
            other.append(pz_ref[t, v, rows, :])
        terms = face_terms(own, other, 2, sign)
        for v in range(5):
            term = terms[v]
            result[v][0][r] = jnp.where(outer, term, 0.0)
            moved = jnp.where(slot == 0, pltpu.roll(term, 7, 0), pltpu.roll(term, 1, 0))
            result[v][1][r] = jnp.where(outer, moved, 0.0)
    return result


def volume_tile(t, states, targets, coef_ref, start, emit, halves=(0, 1)):
    slot = sublanes() % 4
    state, prim = {}, {}
    for a, ref in states.items():
        for r in halves:
            rows = slice(8 * r, 8 * r + 8) if ref.shape[2] == 16 else slice(0, 8)
            state[a, r] = load_state(ref, t, rows)
            prim[a, r] = primitive(state[a, r])

    def flux(a, r, v, direction):
        return flux_entry(state[a, r], prim[a, r][1], prim[a, r][2], v, direction)

    for v in range(5):
        total = {}
        for r in halves:
            column = {a: flux(a, r, v, 0) for a in states}
            for a in targets:
                value = start(v, a, r)
                for other in states:
                    term = float(-DERIV[a, other]) * column[other]
                    value = term if value is None else value + term
                total[a, r] = value
        for a, whole in targets.items():
            if whole:
                first, second = flux(a, 0, v, 1), flux(a, 1, v, 1)
                parts = [first, pltpu.roll(first, 4, 0), second, pltpu.roll(second, 4, 0)]
                for r in range(2):
                    for k in range(4):
                        total[a, r] = total[a, r] - coef_ref[4 * r + k] * parts[k]
            for r in halves:
                acc = total[a, r]
                if whole:
                    along = flux(a, r, v, 2)
                    across = pltpu.roll(along, 4, 0)
                    acc = acc - coef_ref[8] * along
                    for shift in range(1, 4):
                        mixed = pltpu.roll(jnp.where(slot < 4 - shift, along, across), shift, 0)
                        acc = acc - coef_ref[8 + shift] * mixed
                emit(v, a, r, acc)


def sublane_column(values):
    row = sublanes()
    block = jnp.full(VREG, float(values[0]), jnp.float32)
    for s in range(1, 8):
        if values[s] != values[s - 1]:
            block = jnp.where(row >= s, float(values[s]), block)
    return block


def fill_coefficients(coef_ref):
    table = np.zeros((12, 8), np.float32)
    for row in range(8):
        group, c = divmod(row, 4)
        for r in range(2):
            for k in range(4):
                source = 2 * (k // 2) + (group if k % 2 == 0 else 1 - group)
                table[4 * r + k, row] = DERIV[2 * r + group, source]
        for shift in range(4):
            table[8 + shift, row] = DERIV[c, (c - shift) % 4]
    for i in range(12):
        coef_ref[i] = sublane_column(table[i])


def y_face_tile(u_ref, py_ref, r_ref, which, t):
    lower = sublanes() < 4
    sign = jnp.where(lower, -1.0, 1.0).astype(jnp.float32)
    own = [jnp.where(lower, u_ref[t, v, 0:8, :], u_ref[t, v, 8:16, :]) for v in range(5)]
    terms = face_terms(own, [py_ref[t, v] for v in range(5)], 1, sign)
    for v in range(5):
        r_ref[t, v * 2 + which, 0:8, :] += jnp.where(lower, terms[v], 0.0)
        r_ref[t, v * 2 + which, 8:16, :] += jnp.where(lower, 0.0, terms[v])


def x_face_tile(u_ref, other_ref, r_ref, which, t):
    sign = -1.0 if which == 0 else 1.0
    for r in range(2):
        rows = slice(8 * r, 8 * r + 8)
        terms = face_terms(load_state(u_ref, t, rows), load_state(other_ref, t, rows), 0, sign)
        for v in range(5):
            r_ref[t, v * 2 + which, rows, :] += terms[v]


def rates_tile(t, states, pair, sources, pz_ref, py_refs, r_ref, coef_ref, added=None, extra=None):
    targets = {a: True for a in pair}
    refs = [states[a] for a in pair]
    face = z_face_terms(refs, pz_ref, t)

    def start(v, a, r):
        if a not in pair:
            return None
        which = pair.index(a)
        value = face[v][which][r]
        if added is not None:
            value = value + added[t, v * 2 + which, 8 * r : 8 * r + 8, :]
        return value

    def emit(v, a, r, value):
        if a in pair:
            r_ref[t, v * 2 + pair.index(a), 8 * r : 8 * r + 8, :] = value
        else:
            extra[1][t, v * 2 + extra[0].index(a), 8 * r : 8 * r + 8, :] = value

    if extra is not None:
        targets.update({a: False for a in extra[0]})
    volume_tile(t, {a: states[a] for a in sources}, targets, coef_ref, start, emit)
    for which in range(2):
        y_face_tile(refs[which], py_refs[which], r_ref, which, t)


def pack_pair(tiles):
    lane = lanes()
    low = lane < 64
    flip = [[pltpu.roll(half, 64, 1) for half in tile] for tile in tiles]
    first = [
        tiles[0][0],
        tiles[1][0],
        tiles[0][1],
        tiles[1][1],
        jnp.where(low, tiles[2][0], flip[2][1]),
    ]
    second = [
        jnp.where(low, flip[2][0], flip[3][0]),
        jnp.where(low, flip[3][0], flip[4][0]),
        jnp.where(low, flip[2][1], flip[3][1]),
        jnp.where(low, flip[3][1], flip[4][1]),
        jnp.where(low, flip[4][0], tiles[4][1]),
    ]
    return first, second


def unpack_pair(first, second):
    low = lanes() < 64
    flip_first = pltpu.roll(first[4], 64, 1)
    flip = [pltpu.roll(block, 64, 1) for block in second]
    return [
        [first[0], first[2]],
        [first[1], first[3]],
        [jnp.where(low, first[4], flip[0]), jnp.where(low, flip_first, flip[2])],
        [jnp.where(low, flip[0], flip[1]), jnp.where(low, flip[2], flip[3])],
        [jnp.where(low, flip[1], flip[4]), jnp.where(low, flip[3], second[4])],
    ]


PACK_ROWS = 50
HALO_ROWS = 57


def pack_halo_parts(halos):
    lane = lanes()
    packed = [
        jnp.where(lane < 64, halos[2 * v], pltpu.roll(halos[2 * v + 1], 64, 1)) for v in range(5)
    ]
    for first in (0, 8):
        block = None
        for n in range(first, min(first + 8, 10)):
            moved = pltpu.roll(halos[n], (16 * (n - first) + 64) % 128, 1)
            block = moved if block is None else jnp.where(lane < 16 * (n - first), block, moved)
        packed.append(block)
    return packed


def unpack_halo_parts(packed):
    lane = lanes()
    halos = []
    for n in range(10):
        low = packed[n // 2] if n % 2 == 0 else pltpu.roll(packed[n // 2], 64, 1)
        rest = pltpu.roll(packed[5 + n // 8], (64 - 16 * (n % 8)) % 128, 1)
        halos.append(jnp.where(lane < 64, low, rest))
    return halos


def pack_message(load, quarter, put):
    lane = lanes()
    low = lane < 64
    lower = sublanes() < 4
    odd = quarter % 2
    base = (5 * quarter) // 2
    shift = 64 * odd
    keep = lane < 128 - shift
    under = lax.rem(base + 9, 10)
    over = lax.rem(base + 3, 10)
    below_shift = 80 - 64 * odd
    above_shift = 64 - 64 * odd
    halos = [None] * 10
    for v in range(5):
        tops = []
        for r in range(2):
            blocks = [[load(which, v, r, base + i) for i in range(3)] for which in range(2)]
            turned = [[pltpu.roll(x, shift, 1) for x in half] for half in blocks]
            first = (5 * r + v) * 5
            for which in range(2):
                put(first + 2 * which, jnp.where(keep, turned[which][0], turned[which][1]))
                put(first + 2 * which + 1, jnp.where(keep, turned[which][1], turned[which][2]))
            put(first + 4, jnp.where(low, turned[0][2], pltpu.roll(blocks[1][2], above_shift, 1)))
            tops.append(blocks)
        for which in range(2):
            below = jnp.where(
                lane < below_shift,
                pltpu.roll(load(which, v, 1, under), below_shift, 1),
                pltpu.roll(tops[1][which][0], below_shift, 1),
            )
            above = jnp.where(
                lane < above_shift,
                pltpu.roll(tops[0][which][2], above_shift, 1),
                pltpu.roll(load(which, v, 0, over), above_shift, 1),
            )
            halos[2 * v + which] = jnp.where(lower, above, below)
    for i, block in enumerate(pack_halo_parts(halos)):
        put(PACK_ROWS + i, block)


def rate_loader(r_ref):
    return lambda which, v, r, t: r_ref[t, v * 2 + which, 8 * r : 8 * r + 8, :]


def writer(*refs):
    def put(row, block):
        for ref in refs:
            if row < ref.shape[0]:
                ref[row] = block
                return
            row -= ref.shape[0]

    return put


def start_rows(v, a, r, t):
    return pl.ds(((v * 4 + a) * 16 + 8 * r) * 10 + t, 8, stride=10)


def front_kernel(rank_ref, start_hbm, offset_hbm, u0, u1, u2, u3, r_ref, m1, m2, m3, start_ref, offset_ref, pz_ref, py1, py2, coef_ref, sems):
    copies = []
    for v in range(5):
        rows = pl.ds(640 * v, 640)
        pair = [
            pltpu.make_async_copy(start_hbm.at[rows], start_ref.at[rows], sems.at[2 * v]),
            pltpu.make_async_copy(offset_hbm.at[rows], offset_ref.at[rows], sems.at[2 * v + 1]),
        ]
        for copy in pair:
            copy.start()
        copies.append(pair)
    states = {0: u0, 1: u1, 2: u2, 3: u3}
    fill_coefficients(coef_ref)
    for v in range(5):
        for copy in copies[v]:
            copy.wait()
        rows = slice(640 * v, 640 * v + 640)
        offset_ref[rows, :] = offset_ref[rows, :] + start_ref[rows, :]
        for a in range(4):
            for t in range(TILES):
                for r in range(2):
                    states[a][t, v, 8 * r : 8 * r + 8, :] = offset_ref[start_rows(v, a, r, t), :]
        z_partners((u1, u2), pz_ref, v)
        y_partners(u1, py1, None, v)
        y_partners(u2, py2, None, v)

    def one_tile(t, carry):
        rates_tile(t, states, (1, 2), (0, 1, 2, 3), pz_ref, (py1, py2), r_ref, coef_ref)
        return carry

    lax.fori_loop(0, TILES, one_tile, 0)
    for d, out in ((1, m1), (2, m2), (3, m3)):
        pack_message(rate_loader(r_ref), lax.rem(rank_ref[0] + d, 4), writer(out))


def edge_inner_kernel(u0, u1, u2, u3, r_ref, pz_ref, py0, py3, coef_ref):
    fill_coefficients(coef_ref)
    z_partners((u0, u3), pz_ref)
    y_partners(u0, py0)
    y_partners(u3, py3)
    states = {0: u0, 1: u1, 2: u2, 3: u3}

    def one_tile(t, carry):
        rates_tile(t, states, (0, 3), (0, 1, 2, 3), pz_ref, (py0, py3), r_ref, coef_ref)
        return carry

    lax.fori_loop(0, TILES, one_tile, 0)


def add_x_faces(u0, u3, inner_ref, left_ref, right_ref, r_ref):
    def one_tile(t, carry):
        r_ref[t] = inner_ref[t]
        x_face_tile(u0, left_ref, r_ref, 0, t)
        x_face_tile(u3, right_ref, r_ref, 1, t)
        return carry

    lax.fori_loop(0, TILES, one_tile, 0)


def edge_outer_kernel(rank_ref, u0, u3, inner_ref, left_ref, right_ref, m1, m2, m3, r_ref):
    add_x_faces(u0, u3, inner_ref, left_ref, right_ref, r_ref)
    for d, out in ((1, m1), (2, m2), (3, m3)):
        pack_message(rate_loader(r_ref), lax.rem(rank_ref[0] + d, 4), writer(out))


def own_kernel(rank_ref, start_hbm, mid_ref, edge_ref, start_mid, start_edge, own_mid, own_edge, start_ref, sems):
    rank = rank_ref[0]
    copy = pltpu.make_async_copy(start_hbm, start_ref, sems.at[0])
    copy.start()
    copy.wait()
    for pair, rates, start_out, own_out in (((1, 2), mid_ref, start_mid, own_mid), ((0, 3), edge_ref, start_edge, own_edge)):

        def load(which, v, r, t):
            return start_ref[start_rows(v, pair[which], r, t), :]

        pack_message(load, rank, writer(start_out))
        pack_message(rate_loader(rates), rank, writer(own_out))


def node_weights(rank_ref, table_ref):
    rank = rank_ref[0]
    return [[table_ref[m * 4 + lax.rem(rank + 4 - d, 4)] for d in range(4)] for m in range(4)]


def node_state(weight, start_ref, rates, m, row):
    total = start_ref[row]
    for d in range(4):
        total = total + weight[m][d] * rates[d][row]
    return total


def assemble(weight, start_ref, rates, states):
    def one_variable(v, carry):
        for r in range(2):
            first = (5 * r + v) * 5
            for pair in range(2):
                pieces = [
                    [node_state(weight, start_ref, rates, 2 * pair + half, first + i) for i in range(5)]
                    for half in range(2)
                ]
                tiles = unpack_pair(*pieces)
                for i in range(5):
                    for which in range(2):
                        states[which][5 * pair + i, v, 8 * r : 8 * r + 8, :] = tiles[i][which]
        return carry

    lax.fori_loop(0, 5, one_variable, 0)


def assemble_halos(weight, start_ref, rates, halos):
    for m in range(4):
        blocks = unpack_halo_parts(
            [node_state(weight, start_ref, rates, m, PACK_ROWS + i) for i in range(7)]
        )
        for n in range(10):
            halos[n % 2][m, n // 2] = blocks[n]


def send_increments(rank_ref, table_ref, r_ref, halves, outs):
    rank = rank_ref[0]
    weight = [[table_ref[lax.rem(rank + d, 4) * 4 + j] for j in range(4)] for d in range(4)]

    def one_variable(v, carry):
        for place, r in enumerate(halves):
            rows = slice(8 * r, 8 * r + 8) if r_ref.shape[2] == 16 else slice(0, 8)
            pieces = []
            for pair in range(2):
                tiles = [[r_ref[5 * pair + i, 2 * v + which, rows, :] for which in range(2)] for i in range(5)]
                pieces.extend(pack_pair(tiles))
            for d in range(4):
                for i in range(5):
                    total = weight[d][0] * pieces[0][i]
                    for j in range(1, 4):
                        total = total + weight[d][j] * pieces[j][i]
                    outs[d][(5 * place + v) * 5 + i] = total
        return carry

    lax.fori_loop(0, 5, one_variable, 0)


def middle_kernel(rank_ref, table_ref, start_ref, q0, q1, q2, q3, mid_ref, edge_ref, u1, u2, h1, h2, pz_ref, py1, py2, coef_ref):
    fill_coefficients(coef_ref)
    weight = node_weights(rank_ref, table_ref)
    assemble(weight, start_ref, (q0, q1, q2, q3), (u1, u2))
    assemble_halos(weight, start_ref, (q0, q1, q2, q3), (h1, h2))
    z_partners((u1, u2), pz_ref)
    y_partners(u1, py1, h1)
    y_partners(u2, py2, h2)
    states = {1: u1, 2: u2}

    def one_tile(t, carry):
        rates_tile(t, states, (1, 2), (1, 2), pz_ref, (py1, py2), mid_ref, coef_ref, extra=((0, 3), edge_ref))
        return carry

    lax.fori_loop(0, TILES, one_tile, 0)


def join_kernel(rank_ref, table_ref, start_ref, q0, q1, q2, q3, mid_ref, u0, u3, o0, o1, o2, o3, r_ref):
    assemble(node_weights(rank_ref, table_ref), start_ref, (q0, q1, q2, q3), (u0, u3))

    def one_tile(t, carry):
        def start(v, a, r):
            return mid_ref[t, v * 2 + a - 1, 8 * r : 8 * r + 8, :]

        def emit(v, a, r, value):
            r_ref[t, v * 2 + a - 1, 8 * r : 8 * r + 8, :] = value

        volume_tile(t, {0: u0, 3: u3}, {1: False, 2: False}, None, start, emit)
        return carry

    lax.fori_loop(0, TILES, one_tile, 0)
    send_increments(rank_ref, table_ref, r_ref, (0, 1), (o0, o1, o2, o3))


def last_inner_kernel(rank_ref, table_ref, u0, u3, start_ref, q0, q1, q2, q3, partial_ref, r_ref, h0, h3, pz_ref, py0, py3, coef_ref):
    fill_coefficients(coef_ref)
    assemble_halos(node_weights(rank_ref, table_ref), start_ref, (q0, q1, q2, q3), (h0, h3))
    z_partners((u0, u3), pz_ref)
    y_partners(u0, py0, h0)
    y_partners(u3, py3, h3)
    states = {0: u0, 3: u3}

    def one_tile(t, carry):
        rates_tile(t, states, (0, 3), (0, 3), pz_ref, (py0, py3), r_ref, coef_ref, added=partial_ref)
        return carry

    lax.fori_loop(0, TILES, one_tile, 0)


def last_outer_kernel(rank_ref, table_ref, u0, u3, inner_ref, left_ref, right_ref, o0, o1, o2, o3, r_ref):
    add_x_faces(u0, u3, inner_ref, left_ref, right_ref, r_ref)
    send_increments(rank_ref, table_ref, r_ref, (0, 1), (o0, o1, o2, o3))


def finish(rank_ref, pieces, out_hbm, order_ref, stage_ref, sems, pair):
    rank = rank_ref[0]
    for d in range(4):
        order_ref[lax.rem(rank + 4 - d, 4)] = pieces[d][...]
    copies = []
    for v in range(5):
        for r in range(2):
            for half in range(2):
                first = (5 * r + v) * 5
                blocks = [[order_ref[2 * half + k, first + i] for i in range(5)] for k in range(2)]
                tiles = unpack_pair(*blocks)
                for i in range(5):
                    for which in range(2):
                        row = (v * 2 + which) * 160 + 80 * r + 5 * half + i
                        stage_ref[pl.ds(row, 8, stride=10), :] = tiles[i][which]
        for which in range(2):
            n = v * 2 + which
            copy = pltpu.make_async_copy(
                stage_ref.at[pl.ds(n * 160, 160)],
                out_hbm.at[pl.ds((v * 4 + pair[which]) * 160, 160)],
                sems.at[n],
            )
            copy.start()
            copies.append(copy)
    for copy in copies:
        copy.wait()


def finish_middle(rank_ref, q0, q1, q2, q3, out_hbm, order_ref, stage_ref, sems):
    finish(rank_ref, (q0, q1, q2, q3), out_hbm, order_ref, stage_ref, sems, (1, 2))


def finish_edge(rank_ref, q0, q1, q2, q3, before_hbm, out_hbm, order_ref, stage_ref, sems):
    finish(rank_ref, (q0, q1, q2, q3), out_hbm, order_ref, stage_ref, sems, (0, 3))


def f32(*shape):
    return jax.ShapeDtypeStruct(shape, jnp.float32)


TRACE = (TILES, 5, 16, 128)
SIDE = (TILES, 5, 8, 128)
RATE = (TILES, 10, 16, 128)
HALO = (4, 5, 8, 128)
FLAT = (3200, 128)
MESSAGE = (HALO_ROWS, 8, 128)
PIECE = (PACK_ROWS, 8, 128)
COEF = (12, 8, 128)


def call(kernel, outs, args, scratch=(), flops=0, aliases=None):
    place = {
        "s": pl.BlockSpec(memory_space=pltpu.SMEM),
        "v": pl.BlockSpec(memory_space=pltpu.VMEM),
        "h": pl.BlockSpec(memory_space=pltpu.HBM),
    }
    moved = sum(4 * math.prod(a.shape) for _, a in args)
    moved += sum(4 * math.prod(shape) for _, shape in outs)
    result = pl.pallas_call(
        kernel,
        out_shape=[f32(*shape) for _, shape in outs],
        in_specs=[place[where] for where, _ in args],
        out_specs=[place[where] for where, _ in outs],
        scratch_shapes=[
            pltpu.SemaphoreType.DMA(shape) if len(shape) == 1 else pltpu.VMEM(shape, jnp.float32)
            for shape in scratch
        ],
        input_output_aliases=aliases or {},
        compiler_params=pltpu.CompilerParams(vmem_limit_bytes=VMEM_LIMIT),
        cost_estimate=pl.CostEstimate(flops=flops, bytes_accessed=1, transcendentals=0),
    )(*[a for _, a in args])
    return result


def shifted(block, axis, distance):
    count = lax.axis_size(axis)
    return lax.ppermute(block, axis, [((i - distance) % count, i) for i in range(count)])


def v(*arrays):
    return [("v", a) for a in arrays]


def exchange(messages):
    return [shifted(messages[d - 1], "node", d) for d in (1, 2, 3)]


def body(start_state, node_offset):
    start_flat = start_state.reshape(FLAT)
    offset_flat = node_offset.reshape(FLAT)
    rank = ("s", lax.axis_index("node").astype(jnp.int32).reshape(1))
    table = ("s", jnp.asarray(QUAD.reshape(16)))

    u0, u1, u2, u3, mid, *sent = call(
        front_kernel,
        v(TRACE, TRACE, TRACE, TRACE, RATE, MESSAGE, MESSAGE, MESSAGE),
        [rank, ("h", start_flat), ("h", offset_flat)],
        scratch=[FLAT, FLAT, TRACE, SIDE, SIDE, COEF, (10,)],
    )
    got_mid = exchange(sent)
    left = shifted(u3, "space", 1)
    right = shifted(u0, "space", -1)
    (inner,) = call(
        edge_inner_kernel,
        v(RATE),
        v(u0, u1, u2, u3),
        scratch=[TRACE, SIDE, SIDE, COEF],
    )
    *sent, edge = call(
        edge_outer_kernel,
        v(MESSAGE, MESSAGE, MESSAGE, RATE),
        [rank] + v(u0, u3, inner, left, right),
    )
    got_edge = exchange(sent)
    start_mid, start_edge, own_mid, own_edge = call(
        own_kernel,
        v(MESSAGE, MESSAGE, MESSAGE, MESSAGE),
        [rank, ("h", start_flat)] + v(mid, edge),
        scratch=[FLAT, (1,)],
    )
    mid, edge = call(
        middle_kernel,
        v(RATE, RATE),
        [rank, table] + v(start_mid, own_mid, *got_mid),
        scratch=[TRACE, TRACE, HALO, HALO, TRACE, SIDE, SIDE, COEF],
    )
    u0, u3, own_mid, *sent = call(
        join_kernel,
        v(TRACE, TRACE, PIECE, PIECE, PIECE, PIECE),
        [rank, table] + v(start_edge, own_edge, *got_edge, mid),
        scratch=[RATE],
    )
    got_mid = exchange(sent)
    left = shifted(u3, "space", 1)
    right = shifted(u0, "space", -1)
    (inner,) = call(
        last_inner_kernel,
        v(RATE),
        [rank, table] + v(u0, u3, start_edge, own_edge, *got_edge, edge),
        scratch=[HALO, HALO, TRACE, SIDE, SIDE, COEF],
    )
    own_edge, *sent = call(
        last_outer_kernel,
        v(PIECE, PIECE, PIECE, PIECE),
        [rank, table] + v(u0, u3, inner, left, right),
        scratch=[RATE],
    )
    got_edge = exchange(sent)
    finishing = [(4,) + PIECE, (1600, 128), (10,)]
    (result,) = call(
        finish_middle,
        [("h", FLAT)],
        [rank] + v(own_mid, *got_mid),
        scratch=finishing,
    )
    (result,) = call(
        finish_edge,
        [("h", FLAT)],
        [rank] + v(own_edge, *got_edge) + [("h", result)],
        scratch=finishing,
        aliases={5: 0},
    )
    return result.reshape(node_offset.shape)


def solution(mesh):
    return jax.shard_map(
        body,
        mesh=mesh,
        in_specs=(
            P(None, None, None, None, "space", None),
            P("node", None, None, None, None, "space", None),
        ),
        out_specs=P("node", None, None, None, None, "space", None),
        check_vma=False,
    )
```

```python
import functools
import math

import jax
import jax.numpy as jnp
import numpy as np
from jax import lax
from jax.experimental import pallas as pl
from jax.experimental.pallas import tpu as pltpu
from jax.sharding import PartitionSpec as P

EZ = 80
QUARTER = 320
TILES = 10
ITERS = 2
gamma_gas = 1.4
step_length = 0.01
VMEM_LIMIT = 48 * 1024 * 1024
FRONT_LIMIT = 53_000_000


def lobatto_derivative():
    points = np.array([-1.0, -math.sqrt(0.2), math.sqrt(0.2), 1.0])
    barycentric = np.ones(4)
    for i in range(4):
        for k in range(4):
            if k != i:
                barycentric[i] = barycentric[i] / (points[i] - points[k])
    derivative = np.zeros((4, 4))
    for i in range(4):
        for j in range(4):
            if i != j:
                derivative[i, j] = barycentric[j] / barycentric[i] / (points[i] - points[j])
        derivative[i, i] = -np.sum(derivative[i])
    return derivative


def collocation_matrix():
    near_root = math.sqrt(3.0 / 7 - 2.0 / 7 * math.sqrt(1.2))
    far_root = math.sqrt(3.0 / 7 + 2.0 / 7 * math.sqrt(1.2))
    time_nodes = [(1.0 + value) / 2 for value in (-far_root, -near_root, near_root, far_root)]
    quad_table = np.zeros((4, 4))
    for j in range(4):
        coeffs = [1.0]
        for k in range(4):
            if k != j:
                scale = 1.0 / (time_nodes[j] - time_nodes[k])
                widened = [0.0] * (len(coeffs) + 1)
                for power in range(len(coeffs)):
                    widened[power + 1] = widened[power + 1] + coeffs[power] * scale
                    widened[power] = widened[power] - time_nodes[k] * coeffs[power] * scale
                coeffs = widened
        for m in range(4):
            total = 0.0
            for power in range(len(coeffs)):
                total = total + coeffs[power] * time_nodes[m] ** (power + 1) / (power + 1)
            quad_table[m, j] = total
    return quad_table


DERIV = np.float32(lobatto_derivative())
QUAD = np.float32(step_length * collocation_matrix())
VREG = (8, 128)


def lanes():
    return lax.broadcasted_iota(jnp.int32, VREG, 1)


def sublanes():
    return lax.broadcasted_iota(jnp.int32, VREG, 0)


def lane_roll(tiles, shift):
    count = len(tiles)
    whole, rest = divmod(shift % (128 * count), 128)
    if rest == 0:
        return [tiles[(t - whole) % count] for t in range(count)]
    rotated = [pltpu.roll(tile, rest, 1) for tile in tiles]
    lane = lanes()
    return [
        jnp.where(lane < rest, rotated[(t - whole - 1) % count], rotated[(t - whole) % count])
        for t in range(count)
    ]


def primitive(state):
    rho, m1, m2, m3, energy = state
    inverse = 1.0 / rho
    v1, v2, v3 = m1 * inverse, m2 * inverse, m3 * inverse
    pressure = (gamma_gas - 1.0) * (energy - 0.5 * (m1 * v1 + m2 * v2 + m3 * v3))
    return inverse, (v1, v2, v3), pressure


def flux_entry(state, velocity, pressure, variable, direction):
    speed = velocity[direction]
    if variable == 0:
        return state[1 + direction]
    if variable == 4:
        return (state[4] + pressure) * speed
    entry = state[variable] * speed
    if variable - 1 == direction:
        entry = entry + pressure
    return entry


def wave(inverse, velocity, pressure, direction):
    square = gamma_gas * pressure * inverse
    return jnp.abs(velocity[direction]) + square * lax.rsqrt(square)


def face_terms(own, other, direction, sign):
    own_inv, own_v, own_p = primitive(own)
    oth_inv, oth_v, oth_p = primitive(other)
    speed = 3.0 * jnp.maximum(
        wave(own_inv, own_v, own_p, direction), wave(oth_inv, oth_v, oth_p, direction)
    )
    weight = 3.0 * sign
    terms = []
    for variable in range(5):
        jump = other[variable] - own[variable]
        flux_jump = flux_entry(own, own_v, own_p, variable, direction) - flux_entry(
            other, oth_v, oth_p, variable, direction
        )
        terms.append(speed * jump + weight * flux_jump)
    return terms


def z_partners(pair, pz_ref, only=None):
    lane = lanes()
    slot = sublanes() % 4
    even_ref, odd_ref = pair

    def one_variable(v, carry):
        for r in range(2):
            rows = slice(8 * r, 8 * r + 8)
            mixed = []
            for t in range(TILES):
                even = even_ref[t, v, rows, :]
                odd = odd_ref[t, v, rows, :]
                low = jnp.where(slot == 0, pltpu.roll(even, 5, 0), pltpu.roll(odd, 6, 0))
                high = jnp.where(slot == 3, pltpu.roll(even, 3, 0), pltpu.roll(odd, 2, 0))
                mixed.append(jnp.where(slot < 2, low, high))
            before = lane_roll(mixed, 1)
            before_wrap = lane_roll(mixed, -(EZ - 1))
            after = lane_roll(mixed, -1)
            after_wrap = lane_roll(mixed, EZ - 1)
            for t in range(TILES):
                column = (lane + 128 * t) % EZ
                low = jnp.where(column == 0, before_wrap[t], before[t])
                high = jnp.where(column == EZ - 1, after_wrap[t], after[t])
                pz_ref[t, v, rows, :] = jnp.where(slot < 2, low, high)
        return carry

    if only is None:
        lax.fori_loop(0, 5, one_variable, 0)
    else:
        one_variable(only, 0)


def y_partners(u_ref, py_ref, halo_ref=None, only=None):
    lane = lanes()
    lower = sublanes() < 4

    def one_variable(v, carry):
        swapped = []
        for t in range(TILES):
            trace = jnp.where(lower, u_ref[t, v, 0:8, :], u_ref[t, v, 8:16, :])
            swapped.append(pltpu.roll(trace, 4, 0))
        before = lane_roll(swapped, EZ)
        after = lane_roll(swapped, -EZ)
        if halo_ref is not None:
            for m in range(4):
                base = 5 * (m // 2)
                got = pltpu.roll(halo_ref[m, v], 4, 0)
                if m % 2 == 0:
                    before[base] = jnp.where(lane < 80, got, before[base])
                    moved = pltpu.roll(got, 112, 1)
                    after[base + 1] = jnp.where(lane >= 112, moved, after[base + 1])
                    after[base + 2] = jnp.where(lane < 64, moved, after[base + 2])
                else:
                    moved = pltpu.roll(got, 64, 1)
                    before[base + 2] = jnp.where(lane >= 64, moved, before[base + 2])
                    before[base + 3] = jnp.where(lane < 16, moved, before[base + 3])
                    moved = pltpu.roll(got, 48, 1)
                    after[base + 4] = jnp.where(lane >= 48, moved, after[base + 4])
        for t in range(TILES):
            py_ref[t, v] = jnp.where(lower, before[t], after[t])
        return carry

    if only is None:
        lax.fori_loop(0, 5, one_variable, 0)
    else:
        one_variable(only, 0)


def load_state(u_ref, t, rows):
    return [u_ref[t, v, rows, :] for v in range(5)]


def z_face_terms(pair, pz_ref, t):
    slot = sublanes() % 4
    outer = (slot == 0) | (slot == 3)
    sign = jnp.where(slot < 2, -1.0, 1.0).astype(jnp.float32)
    result = [[[None, None] for _ in range(2)] for _ in range(5)]
    for r in range(2):
        rows = slice(8 * r, 8 * r + 8)
        own, other = [], []
        for v in range(5):
            even = pair[0][t, v, rows, :]
            odd = pair[1][t, v, rows, :]
            inner = jnp.where(slot == 1, pltpu.roll(odd, 1, 0), pltpu.roll(odd, 7, 0))
            own.append(jnp.where(outer, even, inner))
            other.append(pz_ref[t, v, rows, :])
        terms = face_terms(own, other, 2, sign)
        for v in range(5):
            term = terms[v]
            result[v][0][r] = jnp.where(outer, term, 0.0)
            moved = jnp.where(slot == 0, pltpu.roll(term, 7, 0), pltpu.roll(term, 1, 0))
            result[v][1][r] = jnp.where(outer, moved, 0.0)
    return result


def volume_tile(t, states, targets, coef_ref, start, emit, halves=(0, 1)):
    slot = sublanes() % 4
    state, prim = {}, {}
    for a, ref in states.items():
        for r in halves:
            rows = slice(8 * r, 8 * r + 8) if ref.shape[2] == 16 else slice(0, 8)
            state[a, r] = load_state(ref, t, rows)
            prim[a, r] = primitive(state[a, r])

    def flux(a, r, v, direction):
        return flux_entry(state[a, r], prim[a, r][1], prim[a, r][2], v, direction)

    for v in range(5):
        total = {}
        for r in halves:
            column = {a: flux(a, r, v, 0) for a in states}
            for a in targets:
                value = start(v, a, r)
                for other in states:
                    term = float(-DERIV[a, other]) * column[other]
                    value = term if value is None else value + term
                total[a, r] = value
        for a, whole in targets.items():
            if whole:
                first, second = flux(a, 0, v, 1), flux(a, 1, v, 1)
                parts = [first, pltpu.roll(first, 4, 0), second, pltpu.roll(second, 4, 0)]
                for r in range(2):
                    for k in range(4):
                        total[a, r] = total[a, r] - coef_ref[4 * r + k] * parts[k]
            for r in halves:
                acc = total[a, r]
                if whole:
                    along = flux(a, r, v, 2)
                    across = pltpu.roll(along, 4, 0)
                    acc = acc - coef_ref[8] * along
                    for shift in range(1, 4):
                        mixed = pltpu.roll(jnp.where(slot < 4 - shift, along, across), shift, 0)
                        acc = acc - coef_ref[8 + shift] * mixed
                emit(v, a, r, acc)


def sublane_column(values):
    row = sublanes()
    block = jnp.full(VREG, float(values[0]), jnp.float32)
    for s in range(1, 8):
        if values[s] != values[s - 1]:
            block = jnp.where(row >= s, float(values[s]), block)
    return block


def fill_coefficients(coef_ref):
    table = np.zeros((12, 8), np.float32)
    for row in range(8):
        group, c = divmod(row, 4)
        for r in range(2):
            for k in range(4):
                source = 2 * (k // 2) + (group if k % 2 == 0 else 1 - group)
                table[4 * r + k, row] = DERIV[2 * r + group, source]
        for shift in range(4):
            table[8 + shift, row] = DERIV[c, (c - shift) % 4]
    for i in range(12):
        coef_ref[i] = sublane_column(table[i])


def y_face_tile(u_ref, py_ref, r_ref, which, t):
    lower = sublanes() < 4
    sign = jnp.where(lower, -1.0, 1.0).astype(jnp.float32)
    own = [jnp.where(lower, u_ref[t, v, 0:8, :], u_ref[t, v, 8:16, :]) for v in range(5)]
    terms = face_terms(own, [py_ref[t, v] for v in range(5)], 1, sign)
    for v in range(5):
        r_ref[t, v * 2 + which, 0:8, :] += jnp.where(lower, terms[v], 0.0)
        r_ref[t, v * 2 + which, 8:16, :] += jnp.where(lower, 0.0, terms[v])


def x_face_tile(u_ref, other_ref, r_ref, which, t):
    sign = -1.0 if which == 0 else 1.0
    for r in range(2):
        rows = slice(8 * r, 8 * r + 8)
        terms = face_terms(load_state(u_ref, t, rows), load_state(other_ref, t, rows), 0, sign)
        for v in range(5):
            r_ref[t, v * 2 + which, rows, :] += terms[v]


def rates_tile(t, states, pair, sources, pz_ref, py_refs, r_ref, coef_ref, added=None, extra=None):
    targets = {a: True for a in pair}
    refs = [states[a] for a in pair]
    face = z_face_terms(refs, pz_ref, t)

    def start(v, a, r):
        if a not in pair:
            return None
        which = pair.index(a)
        value = face[v][which][r]
        if added is not None:
            value = value + added[t, v * 2 + which, 8 * r : 8 * r + 8, :]
        return value

    def emit(v, a, r, value):
        if a in pair:
            r_ref[t, v * 2 + pair.index(a), 8 * r : 8 * r + 8, :] = value
        else:
            extra[1][t, v * 2 + extra[0].index(a), 8 * r : 8 * r + 8, :] = value

    if extra is not None:
        targets.update({a: False for a in extra[0]})
    volume_tile(t, {a: states[a] for a in sources}, targets, coef_ref, start, emit)
    for which in range(2):
        y_face_tile(refs[which], py_refs[which], r_ref, which, t)


def pack_pair(tiles):
    lane = lanes()
    low = lane < 64
    flip = [[pltpu.roll(half, 64, 1) for half in tile] for tile in tiles]
    first = [
        tiles[0][0],
        tiles[1][0],
        tiles[0][1],
        tiles[1][1],
        jnp.where(low, tiles[2][0], flip[2][1]),
    ]
    second = [
        jnp.where(low, flip[2][0], flip[3][0]),
        jnp.where(low, flip[3][0], flip[4][0]),
        jnp.where(low, flip[2][1], flip[3][1]),
        jnp.where(low, flip[3][1], flip[4][1]),
        jnp.where(low, flip[4][0], tiles[4][1]),
    ]
    return first, second


def unpack_pair(first, second):
    low = lanes() < 64
    flip_first = pltpu.roll(first[4], 64, 1)
    flip = [pltpu.roll(block, 64, 1) for block in second]
    return [
        [first[0], first[2]],
        [first[1], first[3]],
        [jnp.where(low, first[4], flip[0]), jnp.where(low, flip_first, flip[2])],
        [jnp.where(low, flip[0], flip[1]), jnp.where(low, flip[2], flip[3])],
        [jnp.where(low, flip[1], flip[4]), jnp.where(low, flip[3], second[4])],
    ]


PACK_ROWS = 50
HALO_ROWS = 57


def pack_halo_parts(halos):
    lane = lanes()
    packed = [
        jnp.where(lane < 64, halos[2 * v], pltpu.roll(halos[2 * v + 1], 64, 1)) for v in range(5)
    ]
    for first in (0, 8):
        block = None
        for n in range(first, min(first + 8, 10)):
            moved = pltpu.roll(halos[n], (16 * (n - first) + 64) % 128, 1)
            block = moved if block is None else jnp.where(lane < 16 * (n - first), block, moved)
        packed.append(block)
    return packed


def unpack_halo_parts(packed):
    lane = lanes()
    halos = []
    for n in range(10):
        low = packed[n // 2] if n % 2 == 0 else pltpu.roll(packed[n // 2], 64, 1)
        rest = pltpu.roll(packed[5 + n // 8], (64 - 16 * (n % 8)) % 128, 1)
        halos.append(jnp.where(lane < 64, low, rest))
    return halos


def pack_message(load, quarter, put):
    lane = lanes()
    low = lane < 64
    lower = sublanes() < 4
    odd = quarter % 2
    base = (5 * quarter) // 2
    shift = 64 * odd
    keep = lane < 128 - shift
    under = lax.rem(base + 9, 10)
    over = lax.rem(base + 3, 10)
    below_shift = 80 - 64 * odd
    above_shift = 64 - 64 * odd
    halos = [None] * 10
    for v in range(5):
        tops = []
        for r in range(2):
            blocks = [[load(which, v, r, base + i) for i in range(3)] for which in range(2)]
            turned = [[pltpu.roll(x, shift, 1) for x in half] for half in blocks]
            first = (5 * r + v) * 5
            for which in range(2):
                put(first + 2 * which, jnp.where(keep, turned[which][0], turned[which][1]))
                put(first + 2 * which + 1, jnp.where(keep, turned[which][1], turned[which][2]))
            put(first + 4, jnp.where(low, turned[0][2], pltpu.roll(blocks[1][2], above_shift, 1)))
            tops.append(blocks)
        for which in range(2):
            below = jnp.where(
                lane < below_shift,
                pltpu.roll(load(which, v, 1, under), below_shift, 1),
                pltpu.roll(tops[1][which][0], below_shift, 1),
            )
            above = jnp.where(
                lane < above_shift,
                pltpu.roll(tops[0][which][2], above_shift, 1),
                pltpu.roll(load(which, v, 0, over), above_shift, 1),
            )
            halos[2 * v + which] = jnp.where(lower, above, below)
    for i, block in enumerate(pack_halo_parts(halos)):
        put(PACK_ROWS + i, block)


def rate_loader(r_ref):
    return lambda which, v, r, t: r_ref[t, v * 2 + which, 8 * r : 8 * r + 8, :]


def writer(*refs):
    def put(row, block):
        for ref in refs:
            if row < ref.shape[0]:
                ref[row] = block
                return
            row -= ref.shape[0]

    return put


def start_rows(v, a, r, t):
    return pl.ds(((v * 4 + a) * 16 + 8 * r) * 10 + t, 8, stride=10)


def front_kernel(rank_ref, start_hbm, offset_hbm, u0, u1, u2, u3, r_ref, m1, m2, m3, start_ref, offset_ref, pz_ref, py1, py2, coef_ref, sems):
    copies = []
    for v in range(5):
        rows = pl.ds(640 * v, 640)
        pair = [
            pltpu.make_async_copy(start_hbm.at[rows], start_ref.at[rows], sems.at[2 * v]),
            pltpu.make_async_copy(offset_hbm.at[rows], offset_ref.at[rows], sems.at[2 * v + 1]),
        ]
        for copy in pair:
            copy.start()
        copies.append(pair)
    states = {0: u0, 1: u1, 2: u2, 3: u3}
    fill_coefficients(coef_ref)
    for v in range(5):
        for copy in copies[v]:
            copy.wait()
        rows = slice(640 * v, 640 * v + 640)
        offset_ref[rows, :] = offset_ref[rows, :] + start_ref[rows, :]
        for a in range(4):
            for t in range(TILES):
                for r in range(2):
                    states[a][t, v, 8 * r : 8 * r + 8, :] = offset_ref[start_rows(v, a, r, t), :]
        z_partners((u1, u2), pz_ref, v)
        y_partners(u1, py1, None, v)
        y_partners(u2, py2, None, v)

    def one_tile(t, carry):
        rates_tile(t, states, (1, 2), (0, 1, 2, 3), pz_ref, (py1, py2), r_ref, coef_ref)
        return carry

    lax.fori_loop(0, TILES, one_tile, 0)
    for d, out in ((1, m1), (2, m2), (3, m3)):
        pack_message(rate_loader(r_ref), lax.rem(rank_ref[0] + d, 4), writer(out))


def edge_inner_kernel(u0, u1, u2, u3, r_ref, pz_ref, py0, py3, coef_ref):
    fill_coefficients(coef_ref)
    z_partners((u0, u3), pz_ref)
    y_partners(u0, py0)
    y_partners(u3, py3)
    states = {0: u0, 1: u1, 2: u2, 3: u3}

    def one_tile(t, carry):
        rates_tile(t, states, (0, 3), (0, 1, 2, 3), pz_ref, (py0, py3), r_ref, coef_ref)
        return carry

    lax.fori_loop(0, TILES, one_tile, 0)


def add_x_faces(u0, u3, inner_ref, left_ref, right_ref, r_ref):
    def one_tile(t, carry):
        r_ref[t] = inner_ref[t]
        x_face_tile(u0, left_ref, r_ref, 0, t)
        x_face_tile(u3, right_ref, r_ref, 1, t)
        return carry

    lax.fori_loop(0, TILES, one_tile, 0)


def edge_outer_kernel(rank_ref, u0, u3, inner_ref, left_ref, right_ref, m1, m2, m3, r_ref):
    add_x_faces(u0, u3, inner_ref, left_ref, right_ref, r_ref)
    for d, out in ((1, m1), (2, m2), (3, m3)):
        pack_message(rate_loader(r_ref), lax.rem(rank_ref[0] + d, 4), writer(out))


def own_kernel(rank_ref, start_hbm, mid_ref, edge_ref, start_mid, start_edge, own_mid, own_edge, start_ref, sems):
    rank = rank_ref[0]
    copy = pltpu.make_async_copy(start_hbm, start_ref, sems.at[0])
    copy.start()
    copy.wait()
    for pair, rates, start_out, own_out in (((1, 2), mid_ref, start_mid, own_mid), ((0, 3), edge_ref, start_edge, own_edge)):

        def load(which, v, r, t):
            return start_ref[start_rows(v, pair[which], r, t), :]

        pack_message(load, rank, writer(start_out))
        pack_message(rate_loader(rates), rank, writer(own_out))


def node_weights(rank_ref, table_ref):
    rank = rank_ref[0]
    return [[table_ref[m * 4 + lax.rem(rank + 4 - d, 4)] for d in range(4)] for m in range(4)]


def node_state(weight, start_ref, rates, m, row):
    total = start_ref[row]
    for d in range(4):
        total = total + weight[m][d] * rates[d][row]
    return total


def assemble(weight, start_ref, rates, states):
    def one_variable(v, carry):
        for r in range(2):
            first = (5 * r + v) * 5
            for pair in range(2):
                pieces = [
                    [node_state(weight, start_ref, rates, 2 * pair + half, first + i) for i in range(5)]
                    for half in range(2)
                ]
                tiles = unpack_pair(*pieces)
                for i in range(5):
                    for which in range(2):
                        states[which][5 * pair + i, v, 8 * r : 8 * r + 8, :] = tiles[i][which]
        return carry

    lax.fori_loop(0, 5, one_variable, 0)


def assemble_halos(weight, start_ref, rates, halos):
    for m in range(4):
        blocks = unpack_halo_parts(
            [node_state(weight, start_ref, rates, m, PACK_ROWS + i) for i in range(7)]
        )
        for n in range(10):
            halos[n % 2][m, n // 2] = blocks[n]


def send_increments(rank_ref, table_ref, r_ref, halves, outs):
    rank = rank_ref[0]
    weight = [[table_ref[lax.rem(rank + d, 4) * 4 + j] for j in range(4)] for d in range(4)]

    def one_variable(v, carry):
        for place, r in enumerate(halves):
            rows = slice(8 * r, 8 * r + 8) if r_ref.shape[2] == 16 else slice(0, 8)
            pieces = []
            for pair in range(2):
                tiles = [[r_ref[5 * pair + i, 2 * v + which, rows, :] for which in range(2)] for i in range(5)]
                pieces.extend(pack_pair(tiles))
            for d in range(4):
                for i in range(5):
                    total = weight[d][0] * pieces[0][i]
                    for j in range(1, 4):
                        total = total + weight[d][j] * pieces[j][i]
                    outs[d][(5 * place + v) * 5 + i] = total
        return carry

    lax.fori_loop(0, 5, one_variable, 0)


def middle_kernel(rank_ref, table_ref, start_ref, q0, q1, q2, q3, mid_ref, edge_ref, u1, u2, h1, h2, pz_ref, py1, py2, coef_ref):
    fill_coefficients(coef_ref)
    weight = node_weights(rank_ref, table_ref)
    assemble(weight, start_ref, (q0, q1, q2, q3), (u1, u2))
    assemble_halos(weight, start_ref, (q0, q1, q2, q3), (h1, h2))
    z_partners((u1, u2), pz_ref)
    y_partners(u1, py1, h1)
    y_partners(u2, py2, h2)
    states = {1: u1, 2: u2}

    def one_tile(t, carry):
        rates_tile(t, states, (1, 2), (1, 2), pz_ref, (py1, py2), mid_ref, coef_ref, extra=((0, 3), edge_ref))
        return carry

    lax.fori_loop(0, TILES, one_tile, 0)


def join_kernel(rank_ref, table_ref, start_ref, q0, q1, q2, q3, mid_ref, u0, u3, o0, o1, o2, o3, r_ref):
    assemble(node_weights(rank_ref, table_ref), start_ref, (q0, q1, q2, q3), (u0, u3))

    def one_tile(t, carry):
        def start(v, a, r):
            return mid_ref[t, v * 2 + a - 1, 8 * r : 8 * r + 8, :]

        def emit(v, a, r, value):
            r_ref[t, v * 2 + a - 1, 8 * r : 8 * r + 8, :] = value

        volume_tile(t, {0: u0, 3: u3}, {1: False, 2: False}, None, start, emit)
        return carry

    lax.fori_loop(0, TILES, one_tile, 0)
    send_increments(rank_ref, table_ref, r_ref, (0, 1), (o0, o1, o2, o3))


def last_inner_kernel(rank_ref, table_ref, u0, u3, start_ref, q0, q1, q2, q3, partial_ref, r_ref, h0, h3, pz_ref, py0, py3, coef_ref):
    fill_coefficients(coef_ref)
    assemble_halos(node_weights(rank_ref, table_ref), start_ref, (q0, q1, q2, q3), (h0, h3))
    z_partners((u0, u3), pz_ref)
    y_partners(u0, py0, h0)
    y_partners(u3, py3, h3)
    states = {0: u0, 3: u3}

    def one_tile(t, carry):
        rates_tile(t, states, (0, 3), (0, 3), pz_ref, (py0, py3), r_ref, coef_ref, added=partial_ref)
        return carry

    lax.fori_loop(0, TILES, one_tile, 0)


def last_outer_kernel(rank_ref, table_ref, u0, u3, inner_ref, left_ref, right_ref, o0, o1, o2, o3, r_ref):
    add_x_faces(u0, u3, inner_ref, left_ref, right_ref, r_ref)
    send_increments(rank_ref, table_ref, r_ref, (0, 1), (o0, o1, o2, o3))


def finish(rank_ref, pieces, out_hbm, order_ref, stage_ref, sems, pair):
    rank = rank_ref[0]
    for d in range(4):
        order_ref[lax.rem(rank + 4 - d, 4)] = pieces[d][...]
    copies = []
    for v in range(5):
        for r in range(2):
            for half in range(2):
                first = (5 * r + v) * 5
                blocks = [[order_ref[2 * half + k, first + i] for i in range(5)] for k in range(2)]
                tiles = unpack_pair(*blocks)
                for i in range(5):
                    for which in range(2):
                        row = (v * 2 + which) * 160 + 80 * r + 5 * half + i
                        stage_ref[pl.ds(row, 8, stride=10), :] = tiles[i][which]
        for which in range(2):
            n = v * 2 + which
            copy = pltpu.make_async_copy(
                stage_ref.at[pl.ds(n * 160, 160)],
                out_hbm.at[pl.ds((v * 4 + pair[which]) * 160, 160)],
                sems.at[n],
            )
            copy.start()
            copies.append(copy)
    for copy in copies:
        copy.wait()


def finish_middle(rank_ref, q0, q1, q2, q3, out_hbm, order_ref, stage_ref, sems):
    finish(rank_ref, (q0, q1, q2, q3), out_hbm, order_ref, stage_ref, sems, (1, 2))


def finish_edge(rank_ref, q0, q1, q2, q3, before_hbm, out_hbm, order_ref, stage_ref, sems):
    finish(rank_ref, (q0, q1, q2, q3), out_hbm, order_ref, stage_ref, sems, (0, 3))


def f32(*shape):
    return jax.ShapeDtypeStruct(shape, jnp.float32)


TRACE = (TILES, 5, 16, 128)
SIDE = (TILES, 5, 8, 128)
RATE = (TILES, 10, 16, 128)
HALO = (4, 5, 8, 128)
FLAT = (3200, 128)
MESSAGE = (HALO_ROWS, 8, 128)
PIECE = (PACK_ROWS, 8, 128)
COEF = (12, 8, 128)


def call(kernel, outs, args, scratch=(), flops=0, aliases=None, limit=VMEM_LIMIT):
    place = {
        "s": pl.BlockSpec(memory_space=pltpu.SMEM),
        "v": pl.BlockSpec(memory_space=pltpu.VMEM),
        "h": pl.BlockSpec(memory_space=pltpu.HBM),
    }
    moved = sum(4 * math.prod(a.shape) for _, a in args)
    moved += sum(4 * math.prod(shape) for _, shape in outs)
    result = pl.pallas_call(
        kernel,
        out_shape=[f32(*shape) for _, shape in outs],
        in_specs=[place[where] for where, _ in args],
        out_specs=[place[where] for where, _ in outs],
        scratch_shapes=[
            pltpu.SemaphoreType.DMA(shape) if len(shape) == 1 else pltpu.VMEM(shape, jnp.float32)
            for shape in scratch
        ],
        input_output_aliases=aliases or {},
        compiler_params=pltpu.CompilerParams(vmem_limit_bytes=limit),
        cost_estimate=pl.CostEstimate(flops=flops, bytes_accessed=1, transcendentals=0),
    )(*[a for _, a in args])
    return result


def shifted(block, axis, distance):
    count = lax.axis_size(axis)
    return lax.ppermute(block, axis, [((i - distance) % count, i) for i in range(count)])


def v(*arrays):
    return [("v", a) for a in arrays]


def exchange(messages):
    return [shifted(messages[d - 1], "node", d) for d in (1, 2, 3)]


def body(start_state, node_offset):
    start_flat = start_state.reshape(FLAT)
    offset_flat = node_offset.reshape(FLAT)
    rank = ("s", lax.axis_index("node").astype(jnp.int32).reshape(1))
    table = ("s", jnp.asarray(QUAD.reshape(16)))

    u0, u1, u2, u3, mid, *sent = call(
        front_kernel,
        v(TRACE, TRACE, TRACE, TRACE, RATE, MESSAGE, MESSAGE, MESSAGE),
        [rank, ("h", start_flat), ("h", offset_flat)],
        scratch=[FLAT, FLAT, TRACE, SIDE, SIDE, COEF, (10,)],
        limit=FRONT_LIMIT,
    )
    got_mid = exchange(sent)
    left = shifted(u3, "space", 1)
    right = shifted(u0, "space", -1)
    (inner,) = call(
        edge_inner_kernel,
        v(RATE),
        v(u0, u1, u2, u3),
        scratch=[TRACE, SIDE, SIDE, COEF],
    )
    *sent, edge = call(
        edge_outer_kernel,
        v(MESSAGE, MESSAGE, MESSAGE, RATE),
        [rank] + v(u0, u3, inner, left, right),
    )
    got_edge = exchange(sent)
    start_mid, start_edge, own_mid, own_edge = call(
        own_kernel,
        v(MESSAGE, MESSAGE, MESSAGE, MESSAGE),
        [rank, ("h", start_flat)] + v(mid, edge),
        scratch=[FLAT, (1,)],
    )
    mid, edge = call(
        middle_kernel,
        v(RATE, RATE),
        [rank, table] + v(start_mid, own_mid, *got_mid),
        scratch=[TRACE, TRACE, HALO, HALO, TRACE, SIDE, SIDE, COEF],
    )
    u0, u3, own_mid, *sent = call(
        join_kernel,
        v(TRACE, TRACE, PIECE, PIECE, PIECE, PIECE),
        [rank, table] + v(start_edge, own_edge, *got_edge, mid),
        scratch=[RATE],
    )
    got_mid = exchange(sent)
    left = shifted(u3, "space", 1)
    right = shifted(u0, "space", -1)
    (inner,) = call(
        last_inner_kernel,
        v(RATE),
        [rank, table] + v(u0, u3, start_edge, own_edge, *got_edge, edge),
        scratch=[HALO, HALO, TRACE, SIDE, SIDE, COEF],
    )
    own_edge, *sent = call(
        last_outer_kernel,
        v(PIECE, PIECE, PIECE, PIECE),
        [rank, table] + v(u0, u3, inner, left, right),
        scratch=[RATE],
    )
    got_edge = exchange(sent)
    finishing = [(4,) + PIECE, (1600, 128), (10,)]
    (result,) = call(
        finish_middle,
        [("h", FLAT)],
        [rank] + v(own_mid, *got_mid),
        scratch=finishing,
    )
    (result,) = call(
        finish_edge,
        [("h", FLAT)],
        [rank] + v(own_edge, *got_edge) + [("h", result)],
        scratch=finishing,
        aliases={5: 0},
    )
    return result.reshape(node_offset.shape)


def solution(mesh):
    return jax.shard_map(
        body,
        mesh=mesh,
        in_specs=(
            P(None, None, None, None, "space", None),
            P("node", None, None, None, None, "space", None),
        ),
        out_specs=P("node", None, None, None, None, "space", None),
        check_vma=False,
    )
```

```python
import functools
import math

import jax
import jax.numpy as jnp
import numpy as np
from jax import lax
from jax.experimental import pallas as pl
from jax.experimental.pallas import tpu as pltpu
from jax.sharding import PartitionSpec as P

EZ = 80
QUARTER = 320
TILES = 10
ITERS = 2
gamma_gas = 1.4
step_length = 0.01
VMEM_LIMIT = 48 * 1024 * 1024
FRONT_LIMIT = 53_000_000


def lobatto_derivative():
    points = np.array([-1.0, -math.sqrt(0.2), math.sqrt(0.2), 1.0])
    barycentric = np.ones(4)
    for i in range(4):
        for k in range(4):
            if k != i:
                barycentric[i] = barycentric[i] / (points[i] - points[k])
    derivative = np.zeros((4, 4))
    for i in range(4):
        for j in range(4):
            if i != j:
                derivative[i, j] = barycentric[j] / barycentric[i] / (points[i] - points[j])
        derivative[i, i] = -np.sum(derivative[i])
    return derivative


def collocation_matrix():
    near_root = math.sqrt(3.0 / 7 - 2.0 / 7 * math.sqrt(1.2))
    far_root = math.sqrt(3.0 / 7 + 2.0 / 7 * math.sqrt(1.2))
    time_nodes = [(1.0 + value) / 2 for value in (-far_root, -near_root, near_root, far_root)]
    quad_table = np.zeros((4, 4))
    for j in range(4):
        coeffs = [1.0]
        for k in range(4):
            if k != j:
                scale = 1.0 / (time_nodes[j] - time_nodes[k])
                widened = [0.0] * (len(coeffs) + 1)
                for power in range(len(coeffs)):
                    widened[power + 1] = widened[power + 1] + coeffs[power] * scale
                    widened[power] = widened[power] - time_nodes[k] * coeffs[power] * scale
                coeffs = widened
        for m in range(4):
            total = 0.0
            for power in range(len(coeffs)):
                total = total + coeffs[power] * time_nodes[m] ** (power + 1) / (power + 1)
            quad_table[m, j] = total
    return quad_table


DERIV = np.float32(lobatto_derivative())
QUAD = np.float32(step_length * collocation_matrix())
VREG = (8, 128)


def lanes():
    return lax.broadcasted_iota(jnp.int32, VREG, 1)


def sublanes():
    return lax.broadcasted_iota(jnp.int32, VREG, 0)


def lane_roll(tiles, shift):
    count = len(tiles)
    whole, rest = divmod(shift % (128 * count), 128)
    if rest == 0:
        return [tiles[(t - whole) % count] for t in range(count)]
    rotated = [pltpu.roll(tile, rest, 1) for tile in tiles]
    lane = lanes()
    return [
        jnp.where(lane < rest, rotated[(t - whole - 1) % count], rotated[(t - whole) % count])
        for t in range(count)
    ]


def primitive(state):
    rho, m1, m2, m3, energy = state
    inverse = 1.0 / rho
    v1, v2, v3 = m1 * inverse, m2 * inverse, m3 * inverse
    pressure = (gamma_gas - 1.0) * (energy - 0.5 * (m1 * v1 + m2 * v2 + m3 * v3))
    return inverse, (v1, v2, v3), pressure


def flux_entry(state, velocity, pressure, variable, direction):
    speed = velocity[direction]
    if variable == 0:
        return state[1 + direction]
    if variable == 4:
        return (state[4] + pressure) * speed
    entry = state[variable] * speed
    if variable - 1 == direction:
        entry = entry + pressure
    return entry


def wave(inverse, velocity, pressure, direction):
    square = gamma_gas * pressure * inverse
    return jnp.abs(velocity[direction]) + square * lax.rsqrt(square)


def face_terms(own, other, direction, sign):
    own_inv, own_v, own_p = primitive(own)
    oth_inv, oth_v, oth_p = primitive(other)
    speed = 3.0 * jnp.maximum(
        wave(own_inv, own_v, own_p, direction), wave(oth_inv, oth_v, oth_p, direction)
    )
    weight = 3.0 * sign
    terms = []
    for variable in range(5):
        jump = other[variable] - own[variable]
        flux_jump = flux_entry(own, own_v, own_p, variable, direction) - flux_entry(
            other, oth_v, oth_p, variable, direction
        )
        terms.append(speed * jump + weight * flux_jump)
    return terms


def z_partners(pair, pz_ref, only=None):
    lane = lanes()
    slot = sublanes() % 4
    even_ref, odd_ref = pair

    def one_variable(v, carry):
        for r in range(2):
            rows = slice(8 * r, 8 * r + 8)
            mixed = []
            for t in range(TILES):
                even = even_ref[t, v, rows, :]
                odd = odd_ref[t, v, rows, :]
                low = jnp.where(slot == 0, pltpu.roll(even, 5, 0), pltpu.roll(odd, 6, 0))
                high = jnp.where(slot == 3, pltpu.roll(even, 3, 0), pltpu.roll(odd, 2, 0))
                mixed.append(jnp.where(slot < 2, low, high))
            before = lane_roll(mixed, 1)
            before_wrap = lane_roll(mixed, -(EZ - 1))
            after = lane_roll(mixed, -1)
            after_wrap = lane_roll(mixed, EZ - 1)
            for t in range(TILES):
                column = (lane + 128 * t) % EZ
                low = jnp.where(column == 0, before_wrap[t], before[t])
                high = jnp.where(column == EZ - 1, after_wrap[t], after[t])
                pz_ref[t, v, rows, :] = jnp.where(slot < 2, low, high)
        return carry

    if only is None:
        lax.fori_loop(0, 5, one_variable, 0)
    else:
        one_variable(only, 0)


def y_partners(u_ref, py_ref, halo_ref=None, only=None):
    lane = lanes()
    lower = sublanes() < 4

    def one_variable(v, carry):
        swapped = []
        for t in range(TILES):
            trace = jnp.where(lower, u_ref[t, v, 0:8, :], u_ref[t, v, 8:16, :])
            swapped.append(pltpu.roll(trace, 4, 0))
        before = lane_roll(swapped, EZ)
        after = lane_roll(swapped, -EZ)
        if halo_ref is not None:
            for m in range(4):
                base = 5 * (m // 2)
                got = pltpu.roll(halo_ref[m, v], 4, 0)
                if m % 2 == 0:
                    before[base] = jnp.where(lane < 80, got, before[base])
                    moved = pltpu.roll(got, 112, 1)
                    after[base + 1] = jnp.where(lane >= 112, moved, after[base + 1])
                    after[base + 2] = jnp.where(lane < 64, moved, after[base + 2])
                else:
                    moved = pltpu.roll(got, 64, 1)
                    before[base + 2] = jnp.where(lane >= 64, moved, before[base + 2])
                    before[base + 3] = jnp.where(lane < 16, moved, before[base + 3])
                    moved = pltpu.roll(got, 48, 1)
                    after[base + 4] = jnp.where(lane >= 48, moved, after[base + 4])
        for t in range(TILES):
            py_ref[t, v] = jnp.where(lower, before[t], after[t])
        return carry

    if only is None:
        lax.fori_loop(0, 5, one_variable, 0)
    else:
        one_variable(only, 0)


def load_state(u_ref, t, rows):
    return [u_ref[t, v, rows, :] for v in range(5)]


def z_face_terms(pair, pz_ref, t):
    slot = sublanes() % 4
    outer = (slot == 0) | (slot == 3)
    sign = jnp.where(slot < 2, -1.0, 1.0).astype(jnp.float32)
    result = [[[None, None] for _ in range(2)] for _ in range(5)]
    for r in range(2):
        rows = slice(8 * r, 8 * r + 8)
        own, other = [], []
        for v in range(5):
            even = pair[0][t, v, rows, :]
            odd = pair[1][t, v, rows, :]
            inner = jnp.where(slot == 1, pltpu.roll(odd, 1, 0), pltpu.roll(odd, 7, 0))
            own.append(jnp.where(outer, even, inner))
            other.append(pz_ref[t, v, rows, :])
        terms = face_terms(own, other, 2, sign)
        for v in range(5):
            term = terms[v]
            result[v][0][r] = jnp.where(outer, term, 0.0)
            moved = jnp.where(slot == 0, pltpu.roll(term, 7, 0), pltpu.roll(term, 1, 0))
            result[v][1][r] = jnp.where(outer, moved, 0.0)
    return result


def volume_tile(t, states, targets, coef_ref, start, emit, halves=(0, 1)):
    slot = sublanes() % 4
    state, prim = {}, {}
    for a, ref in states.items():
        for r in halves:
            rows = slice(8 * r, 8 * r + 8) if ref.shape[2] == 16 else slice(0, 8)
            state[a, r] = load_state(ref, t, rows)
            prim[a, r] = primitive(state[a, r])

    def flux(a, r, v, direction):
        return flux_entry(state[a, r], prim[a, r][1], prim[a, r][2], v, direction)

    for v in range(5):
        total = {}
        for r in halves:
            column = {a: flux(a, r, v, 0) for a in states}
            for a in targets:
                value = start(v, a, r)
                for other in states:
                    term = float(-DERIV[a, other]) * column[other]
                    value = term if value is None else value + term
                total[a, r] = value
        for a, whole in targets.items():
            if whole:
                first, second = flux(a, 0, v, 1), flux(a, 1, v, 1)
                parts = [first, pltpu.roll(first, 4, 0), second, pltpu.roll(second, 4, 0)]
                for r in range(2):
                    for k in range(4):
                        total[a, r] = total[a, r] - coef_ref[4 * r + k] * parts[k]
            for r in halves:
                acc = total[a, r]
                if whole:
                    along = flux(a, r, v, 2)
                    across = pltpu.roll(along, 4, 0)
                    acc = acc - coef_ref[8] * along
                    for shift in range(1, 4):
                        mixed = pltpu.roll(jnp.where(slot < 4 - shift, along, across), shift, 0)
                        acc = acc - coef_ref[8 + shift] * mixed
                emit(v, a, r, acc)


def sublane_column(values):
    row = sublanes()
    block = jnp.full(VREG, float(values[0]), jnp.float32)
    for s in range(1, 8):
        if values[s] != values[s - 1]:
            block = jnp.where(row >= s, float(values[s]), block)
    return block


def fill_coefficients(coef_ref):
    table = np.zeros((12, 8), np.float32)
    for row in range(8):
        group, c = divmod(row, 4)
        for r in range(2):
            for k in range(4):
                source = 2 * (k // 2) + (group if k % 2 == 0 else 1 - group)
                table[4 * r + k, row] = DERIV[2 * r + group, source]
        for shift in range(4):
            table[8 + shift, row] = DERIV[c, (c - shift) % 4]
    for i in range(12):
        coef_ref[i] = sublane_column(table[i])


def y_face_tile(u_ref, py_ref, r_ref, which, t):
    lower = sublanes() < 4
    sign = jnp.where(lower, -1.0, 1.0).astype(jnp.float32)
    own = [jnp.where(lower, u_ref[t, v, 0:8, :], u_ref[t, v, 8:16, :]) for v in range(5)]
    terms = face_terms(own, [py_ref[t, v] for v in range(5)], 1, sign)
    for v in range(5):
        r_ref[t, v * 2 + which, 0:8, :] += jnp.where(lower, terms[v], 0.0)
        r_ref[t, v * 2 + which, 8:16, :] += jnp.where(lower, 0.0, terms[v])


def x_face_tile(u_ref, other_ref, r_ref, which, t):
    sign = -1.0 if which == 0 else 1.0
    for r in range(2):
        rows = slice(8 * r, 8 * r + 8)
        terms = face_terms(load_state(u_ref, t, rows), load_state(other_ref, t, rows), 0, sign)
        for v in range(5):
            r_ref[t, v * 2 + which, rows, :] += terms[v]


def rates_tile(t, states, pair, sources, pz_ref, py_refs, r_ref, coef_ref, added=None, extra=None):
    targets = {a: True for a in pair}
    refs = [states[a] for a in pair]
    face = z_face_terms(refs, pz_ref, t)

    def start(v, a, r):
        if a not in pair:
            return None
        which = pair.index(a)
        value = face[v][which][r]
        if added is not None:
            value = value + added[t, v * 2 + which, 8 * r : 8 * r + 8, :]
        return value

    def emit(v, a, r, value):
        if a in pair:
            r_ref[t, v * 2 + pair.index(a), 8 * r : 8 * r + 8, :] = value
        else:
            extra[1][t, v * 2 + extra[0].index(a), 8 * r : 8 * r + 8, :] = value

    if extra is not None:
        targets.update({a: False for a in extra[0]})
    volume_tile(t, {a: states[a] for a in sources}, targets, coef_ref, start, emit)
    for which in range(2):
        y_face_tile(refs[which], py_refs[which], r_ref, which, t)


def pack_pair(tiles):
    lane = lanes()
    low = lane < 64
    flip = [[pltpu.roll(half, 64, 1) for half in tile] for tile in tiles]
    first = [
        tiles[0][0],
        tiles[1][0],
        tiles[0][1],
        tiles[1][1],
        jnp.where(low, tiles[2][0], flip[2][1]),
    ]
    second = [
        jnp.where(low, flip[2][0], flip[3][0]),
        jnp.where(low, flip[3][0], flip[4][0]),
        jnp.where(low, flip[2][1], flip[3][1]),
        jnp.where(low, flip[3][1], flip[4][1]),
        jnp.where(low, flip[4][0], tiles[4][1]),
    ]
    return first, second


def unpack_pair(first, second):
    low = lanes() < 64
    flip_first = pltpu.roll(first[4], 64, 1)
    flip = [pltpu.roll(block, 64, 1) for block in second]
    return [
        [first[0], first[2]],
        [first[1], first[3]],
        [jnp.where(low, first[4], flip[0]), jnp.where(low, flip_first, flip[2])],
        [jnp.where(low, flip[0], flip[1]), jnp.where(low, flip[2], flip[3])],
        [jnp.where(low, flip[1], flip[4]), jnp.where(low, flip[3], second[4])],
    ]


PACK_ROWS = 50
HALO_ROWS = 57


def pack_halo_parts(halos):
    lane = lanes()
    packed = [
        jnp.where(lane < 64, halos[2 * v], pltpu.roll(halos[2 * v + 1], 64, 1)) for v in range(5)
    ]
    for first in (0, 8):
        block = None
        for n in range(first, min(first + 8, 10)):
            moved = pltpu.roll(halos[n], (16 * (n - first) + 64) % 128, 1)
            block = moved if block is None else jnp.where(lane < 16 * (n - first), block, moved)
        packed.append(block)
    return packed


def unpack_halo_parts(packed):
    lane = lanes()
    halos = []
    for n in range(10):
        low = packed[n // 2] if n % 2 == 0 else pltpu.roll(packed[n // 2], 64, 1)
        rest = pltpu.roll(packed[5 + n // 8], (64 - 16 * (n % 8)) % 128, 1)
        halos.append(jnp.where(lane < 64, low, rest))
    return halos


def pack_message(load, quarter, put):
    lane = lanes()
    low = lane < 64
    lower = sublanes() < 4
    odd = quarter % 2
    base = (5 * quarter) // 2
    shift = 64 * odd
    keep = lane < 128 - shift
    under = lax.rem(base + 9, 10)
    over = lax.rem(base + 3, 10)
    below_shift = 80 - 64 * odd
    above_shift = 64 - 64 * odd
    halos = [None] * 10
    for v in range(5):
        tops = []
        for r in range(2):
            blocks = [[load(which, v, r, base + i) for i in range(3)] for which in range(2)]
            turned = [[pltpu.roll(x, shift, 1) for x in half] for half in blocks]
            first = (5 * r + v) * 5
            for which in range(2):
                put(first + 2 * which, jnp.where(keep, turned[which][0], turned[which][1]))
                put(first + 2 * which + 1, jnp.where(keep, turned[which][1], turned[which][2]))
            put(first + 4, jnp.where(low, turned[0][2], pltpu.roll(blocks[1][2], above_shift, 1)))
            tops.append(blocks)
        for which in range(2):
            below = jnp.where(
                lane < below_shift,
                pltpu.roll(load(which, v, 1, under), below_shift, 1),
                pltpu.roll(tops[1][which][0], below_shift, 1),
            )
            above = jnp.where(
                lane < above_shift,
                pltpu.roll(tops[0][which][2], above_shift, 1),
                pltpu.roll(load(which, v, 0, over), above_shift, 1),
            )
            halos[2 * v + which] = jnp.where(lower, above, below)
    for i, block in enumerate(pack_halo_parts(halos)):
        put(PACK_ROWS + i, block)


def rate_loader(r_ref):
    return lambda which, v, r, t: r_ref[t, v * 2 + which, 8 * r : 8 * r + 8, :]


def writer(*refs):
    def put(row, block):
        for ref in refs:
            if row < ref.shape[0]:
                ref[row] = block
                return
            row -= ref.shape[0]

    return put


def start_rows(v, a, r, t):
    return pl.ds(((v * 4 + a) * 16 + 8 * r) * 10 + t, 8, stride=10)


def front_kernel(rank_ref, start_hbm, offset_hbm, u0, u1, u2, u3, r_ref, m1, m2, m3, start_ref, offset_ref, pz_ref, py1, py2, coef_ref, sems):
    copies = []
    for v in range(5):
        rows = pl.ds(640 * v, 640)
        pair = [
            pltpu.make_async_copy(start_hbm.at[rows], start_ref.at[rows], sems.at[2 * v]),
            pltpu.make_async_copy(offset_hbm.at[rows], offset_ref.at[rows], sems.at[2 * v + 1]),
        ]
        for copy in pair:
            copy.start()
        copies.append(pair)
    states = {0: u0, 1: u1, 2: u2, 3: u3}
    fill_coefficients(coef_ref)
    for v in range(5):
        for copy in copies[v]:
            copy.wait()
        rows = slice(640 * v, 640 * v + 640)
        offset_ref[rows, :] = offset_ref[rows, :] + start_ref[rows, :]
        for a in range(4):
            for t in range(TILES):
                for r in range(2):
                    states[a][t, v, 8 * r : 8 * r + 8, :] = offset_ref[start_rows(v, a, r, t), :]
        z_partners((u1, u2), pz_ref, v)
        y_partners(u1, py1, None, v)
        y_partners(u2, py2, None, v)

    def one_tile(t, carry):
        rates_tile(t, states, (1, 2), (0, 1, 2, 3), pz_ref, (py1, py2), r_ref, coef_ref)
        return carry

    lax.fori_loop(0, TILES, one_tile, 0)
    for d, out in ((1, m1), (2, m2), (3, m3)):
        pack_message(rate_loader(r_ref), lax.rem(rank_ref[0] + d, 4), writer(out))


def edge_inner_kernel(u0, u1, u2, u3, r_ref, pz_ref, py0, py3, coef_ref):
    fill_coefficients(coef_ref)
    z_partners((u0, u3), pz_ref)
    y_partners(u0, py0)
    y_partners(u3, py3)
    states = {0: u0, 1: u1, 2: u2, 3: u3}

    def one_tile(t, carry):
        rates_tile(t, states, (0, 3), (0, 1, 2, 3), pz_ref, (py0, py3), r_ref, coef_ref)
        return carry

    lax.fori_loop(0, TILES, one_tile, 0)


def add_x_faces(u0, u3, inner_ref, left_ref, right_ref, r_ref):
    def one_tile(t, carry):
        r_ref[t] = inner_ref[t]
        x_face_tile(u0, left_ref, r_ref, 0, t)
        x_face_tile(u3, right_ref, r_ref, 1, t)
        return carry

    lax.fori_loop(0, TILES, one_tile, 0)


def edge_outer_kernel(rank_ref, u0, u3, inner_ref, left_ref, right_ref, m1, m2, m3, r_ref):
    add_x_faces(u0, u3, inner_ref, left_ref, right_ref, r_ref)
    for d, out in ((1, m1), (2, m2), (3, m3)):
        pack_message(rate_loader(r_ref), lax.rem(rank_ref[0] + d, 4), writer(out))


def own_kernel(rank_ref, start_hbm, mid_ref, edge_ref, start_mid, start_edge, own_mid, own_edge, start_ref, sems):
    rank = rank_ref[0]
    copy = pltpu.make_async_copy(start_hbm, start_ref, sems.at[0])
    copy.start()
    copy.wait()
    for pair, rates, start_out, own_out in (((1, 2), mid_ref, start_mid, own_mid), ((0, 3), edge_ref, start_edge, own_edge)):

        def load(which, v, r, t):
            return start_ref[start_rows(v, pair[which], r, t), :]

        pack_message(load, rank, writer(start_out))
        pack_message(rate_loader(rates), rank, writer(own_out))


def node_weights(rank_ref, table_ref):
    rank = rank_ref[0]
    return [[table_ref[m * 4 + lax.rem(rank + 4 - d, 4)] for d in range(4)] for m in range(4)]


def node_state(weight, start_ref, rates, m, row):
    total = start_ref[row]
    for d in range(4):
        total = total + weight[m][d] * rates[d][row]
    return total


def assemble(weight, start_ref, rates, states):
    def one_variable(v, carry):
        for r in range(2):
            first = (5 * r + v) * 5
            for pair in range(2):
                pieces = [
                    [node_state(weight, start_ref, rates, 2 * pair + half, first + i) for i in range(5)]
                    for half in range(2)
                ]
                tiles = unpack_pair(*pieces)
                for i in range(5):
                    for which in range(2):
                        states[which][5 * pair + i, v, 8 * r : 8 * r + 8, :] = tiles[i][which]
        return carry

    lax.fori_loop(0, 5, one_variable, 0, unroll=True)


def assemble_halos(weight, start_ref, rates, halos):
    for m in range(4):
        blocks = unpack_halo_parts(
            [node_state(weight, start_ref, rates, m, PACK_ROWS + i) for i in range(7)]
        )
        for n in range(10):
            halos[n % 2][m, n // 2] = blocks[n]


def send_increments(rank_ref, table_ref, r_ref, halves, outs):
    rank = rank_ref[0]
    weight = [[table_ref[lax.rem(rank + d, 4) * 4 + j] for j in range(4)] for d in range(4)]

    def one_variable(v, carry):
        for place, r in enumerate(halves):
            rows = slice(8 * r, 8 * r + 8) if r_ref.shape[2] == 16 else slice(0, 8)
            pieces = []
            for pair in range(2):
                tiles = [[r_ref[5 * pair + i, 2 * v + which, rows, :] for which in range(2)] for i in range(5)]
                pieces.extend(pack_pair(tiles))
            for d in range(4):
                for i in range(5):
                    total = weight[d][0] * pieces[0][i]
                    for j in range(1, 4):
                        total = total + weight[d][j] * pieces[j][i]
                    outs[d][(5 * place + v) * 5 + i] = total
        return carry

    lax.fori_loop(0, 5, one_variable, 0, unroll=True)


def middle_kernel(rank_ref, table_ref, start_ref, q0, q1, q2, q3, mid_ref, edge_ref, u1, u2, h1, h2, pz_ref, py1, py2, coef_ref):
    fill_coefficients(coef_ref)
    weight = node_weights(rank_ref, table_ref)
    assemble(weight, start_ref, (q0, q1, q2, q3), (u1, u2))
    assemble_halos(weight, start_ref, (q0, q1, q2, q3), (h1, h2))
    z_partners((u1, u2), pz_ref)
    y_partners(u1, py1, h1)
    y_partners(u2, py2, h2)
    states = {1: u1, 2: u2}

    def one_tile(t, carry):
        rates_tile(t, states, (1, 2), (1, 2), pz_ref, (py1, py2), mid_ref, coef_ref, extra=((0, 3), edge_ref))
        return carry

    lax.fori_loop(0, TILES, one_tile, 0)


def join_kernel(rank_ref, table_ref, start_ref, q0, q1, q2, q3, mid_ref, u0, u3, o0, o1, o2, o3, r_ref):
    assemble(node_weights(rank_ref, table_ref), start_ref, (q0, q1, q2, q3), (u0, u3))

    def one_tile(t, carry):
        def start(v, a, r):
            return mid_ref[t, v * 2 + a - 1, 8 * r : 8 * r + 8, :]

        def emit(v, a, r, value):
            r_ref[t, v * 2 + a - 1, 8 * r : 8 * r + 8, :] = value

        volume_tile(t, {0: u0, 3: u3}, {1: False, 2: False}, None, start, emit)
        return carry

    lax.fori_loop(0, TILES, one_tile, 0, unroll=5)
    send_increments(rank_ref, table_ref, r_ref, (0, 1), (o0, o1, o2, o3))


def last_inner_kernel(rank_ref, table_ref, u0, u3, start_ref, q0, q1, q2, q3, partial_ref, r_ref, h0, h3, pz_ref, py0, py3, coef_ref):
    fill_coefficients(coef_ref)
    assemble_halos(node_weights(rank_ref, table_ref), start_ref, (q0, q1, q2, q3), (h0, h3))
    z_partners((u0, u3), pz_ref)
    y_partners(u0, py0, h0)
    y_partners(u3, py3, h3)
    states = {0: u0, 3: u3}

    def one_tile(t, carry):
        rates_tile(t, states, (0, 3), (0, 3), pz_ref, (py0, py3), r_ref, coef_ref, added=partial_ref)
        return carry

    lax.fori_loop(0, TILES, one_tile, 0)


def last_outer_kernel(rank_ref, table_ref, u0, u3, inner_ref, left_ref, right_ref, o0, o1, o2, o3, r_ref):
    add_x_faces(u0, u3, inner_ref, left_ref, right_ref, r_ref)
    send_increments(rank_ref, table_ref, r_ref, (0, 1), (o0, o1, o2, o3))


def finish(rank_ref, pieces, out_hbm, order_ref, stage_ref, sems, pair):
    rank = rank_ref[0]
    for d in range(4):
        order_ref[lax.rem(rank + 4 - d, 4)] = pieces[d][...]
    copies = []
    for v in range(5):
        for r in range(2):
            for half in range(2):
                first = (5 * r + v) * 5
                blocks = [[order_ref[2 * half + k, first + i] for i in range(5)] for k in range(2)]
                tiles = unpack_pair(*blocks)
                for i in range(5):
                    for which in range(2):
                        row = (v * 2 + which) * 160 + 80 * r + 5 * half + i
                        stage_ref[pl.ds(row, 8, stride=10), :] = tiles[i][which]
        for which in range(2):
            n = v * 2 + which
            copy = pltpu.make_async_copy(
                stage_ref.at[pl.ds(n * 160, 160)],
                out_hbm.at[pl.ds((v * 4 + pair[which]) * 160, 160)],
                sems.at[n],
            )
            copy.start()
            copies.append(copy)
    for copy in copies:
        copy.wait()


def finish_middle(rank_ref, q0, q1, q2, q3, out_hbm, order_ref, stage_ref, sems):
    finish(rank_ref, (q0, q1, q2, q3), out_hbm, order_ref, stage_ref, sems, (1, 2))


def finish_edge(rank_ref, q0, q1, q2, q3, before_hbm, out_hbm, order_ref, stage_ref, sems):
    finish(rank_ref, (q0, q1, q2, q3), out_hbm, order_ref, stage_ref, sems, (0, 3))


def f32(*shape):
    return jax.ShapeDtypeStruct(shape, jnp.float32)


TRACE = (TILES, 5, 16, 128)
SIDE = (TILES, 5, 8, 128)
RATE = (TILES, 10, 16, 128)
HALO = (4, 5, 8, 128)
FLAT = (3200, 128)
MESSAGE = (HALO_ROWS, 8, 128)
PIECE = (PACK_ROWS, 8, 128)
COEF = (12, 8, 128)


def call(kernel, outs, args, scratch=(), flops=0, aliases=None, limit=VMEM_LIMIT):
    place = {
        "s": pl.BlockSpec(memory_space=pltpu.SMEM),
        "v": pl.BlockSpec(memory_space=pltpu.VMEM),
        "h": pl.BlockSpec(memory_space=pltpu.HBM),
    }
    moved = sum(4 * math.prod(a.shape) for _, a in args)
    moved += sum(4 * math.prod(shape) for _, shape in outs)
    result = pl.pallas_call(
        kernel,
        out_shape=[f32(*shape) for _, shape in outs],
        in_specs=[place[where] for where, _ in args],
        out_specs=[place[where] for where, _ in outs],
        scratch_shapes=[
            pltpu.SemaphoreType.DMA(shape) if len(shape) == 1 else pltpu.VMEM(shape, jnp.float32)
            for shape in scratch
        ],
        input_output_aliases=aliases or {},
        compiler_params=pltpu.CompilerParams(vmem_limit_bytes=limit),
        cost_estimate=pl.CostEstimate(flops=flops, bytes_accessed=1, transcendentals=0),
    )(*[a for _, a in args])
    return result


def shifted(block, axis, distance):
    count = lax.axis_size(axis)
    return lax.ppermute(block, axis, [((i - distance) % count, i) for i in range(count)])


def v(*arrays):
    return [("v", a) for a in arrays]


def exchange(messages):
    return [shifted(messages[d - 1], "node", d) for d in (1, 2, 3)]


def body(start_state, node_offset):
    start_flat = start_state.reshape(FLAT)
    offset_flat = node_offset.reshape(FLAT)
    rank = ("s", lax.axis_index("node").astype(jnp.int32).reshape(1))
    table = ("s", jnp.asarray(QUAD.reshape(16)))

    u0, u1, u2, u3, mid, *sent = call(
        front_kernel,
        v(TRACE, TRACE, TRACE, TRACE, RATE, MESSAGE, MESSAGE, MESSAGE),
        [rank, ("h", start_flat), ("h", offset_flat)],
        scratch=[FLAT, FLAT, TRACE, SIDE, SIDE, COEF, (10,)],
        limit=FRONT_LIMIT,
    )
    got_mid = exchange(sent)
    left = shifted(u3, "space", 1)
    right = shifted(u0, "space", -1)
    (inner,) = call(
        edge_inner_kernel,
        v(RATE),
        v(u0, u1, u2, u3),
        scratch=[TRACE, SIDE, SIDE, COEF],
    )
    *sent, edge = call(
        edge_outer_kernel,
        v(MESSAGE, MESSAGE, MESSAGE, RATE),
        [rank] + v(u0, u3, inner, left, right),
    )
    got_edge = exchange(sent)
    start_mid, start_edge, own_mid, own_edge = call(
        own_kernel,
        v(MESSAGE, MESSAGE, MESSAGE, MESSAGE),
        [rank, ("h", start_flat)] + v(mid, edge),
        scratch=[FLAT, (1,)],
    )
    mid, edge = call(
        middle_kernel,
        v(RATE, RATE),
        [rank, table] + v(start_mid, own_mid, *got_mid),
        scratch=[TRACE, TRACE, HALO, HALO, TRACE, SIDE, SIDE, COEF],
    )
    u0, u3, own_mid, *sent = call(
        join_kernel,
        v(TRACE, TRACE, PIECE, PIECE, PIECE, PIECE),
        [rank, table] + v(start_edge, own_edge, *got_edge, mid),
        scratch=[RATE],
    )
    got_mid = exchange(sent)
    left = shifted(u3, "space", 1)
    right = shifted(u0, "space", -1)
    (inner,) = call(
        last_inner_kernel,
        v(RATE),
        [rank, table] + v(u0, u3, start_edge, own_edge, *got_edge, edge),
        scratch=[HALO, HALO, TRACE, SIDE, SIDE, COEF],
    )
    own_edge, *sent = call(
        last_outer_kernel,
        v(PIECE, PIECE, PIECE, PIECE),
        [rank, table] + v(u0, u3, inner, left, right),
        scratch=[RATE],
    )
    got_edge = exchange(sent)
    finishing = [(4,) + PIECE, (1600, 128), (10,)]
    (result,) = call(
        finish_middle,
        [("h", FLAT)],
        [rank] + v(own_mid, *got_mid),
        scratch=finishing,
    )
    (result,) = call(
        finish_edge,
        [("h", FLAT)],
        [rank] + v(own_edge, *got_edge) + [("h", result)],
        scratch=finishing,
        aliases={5: 0},
    )
    return result.reshape(node_offset.shape)


def solution(mesh):
    return jax.shard_map(
        body,
        mesh=mesh,
        in_specs=(
            P(None, None, None, None, "space", None),
            P("node", None, None, None, None, "space", None),
        ),
        out_specs=P("node", None, None, None, None, "space", None),
        check_vma=False,
    )
```
